32 devices in a mesh: lat: 4 (over y, core), lon: 8 (over z, x).
Axes of the slice: x: 2, y: 2, z: 4, core: 2. Of those that a mesh axis runs over, the one named last changes fastest.
Arguments:
- grid_in: bfloat16 [65536, 227], P(('lat', 'lon')), may hold values from -6 to 6
- mesh_emb: bfloat16 [16384, 512], P(('lat', 'lon')), may hold values from -6 to 6
- enc_dest: int32 [65536, 2], P(('lat', 'lon')), may hold values from 0 to 31, as said below
- enc_node: int32 [65536, 2], P(('lat', 'lon')), may hold values from 0 to 511
- enc_dist: float32 [65536, 2], P(('lat', 'lon')), may hold values from 0.2 to 2
- dec_dist: float32 [65536, 2], P(('lat', 'lon')), may hold values from 0.2 to 2
- mesh_src: int32 [16384, 8], P(('lat', 'lon')), may hold values from 0 to 16383, as said below
- proc_dist: float32 [16384, 8], P(('lat', 'lon')), may hold values from 0.2 to 2
- w_grid_in: bfloat16 [227, 512], replicated, may hold values from -0.375 to 0.375
- w_enc_src: bfloat16 [512, 512], replicated, may hold values from -0.25 to 0.25
- w_enc_dist: float32 [512], replicated, may hold values from -6 to 6
- w_mesh_self: bfloat16 [512, 512], replicated, may hold values from -0.25 to 0.25
- w_mesh_agg: bfloat16 [512, 512], replicated, may hold values from -0.09375 to 0.09375
- w_proc_send: bfloat16 [512, 512], replicated, may hold values from -0.25 to 0.25
- w_proc_recv: bfloat16 [512, 512], replicated, may hold values from -0.25 to 0.25
- w_proc_dist: float32 [512], replicated, may hold values from -6 to 6
- w_proc_self: bfloat16 [512, 512], replicated, may hold values from -0.25 to 0.25
- w_proc_agg: bfloat16 [512, 512], replicated, may hold values from -0.125 to 0.125
- w_dec_send: bfloat16 [512, 512], replicated, may hold values from -0.25 to 0.25
- w_dec_recv: bfloat16 [512, 512], replicated, may hold values from -0.25 to 0.25
- w_dec_dist: float32 [512], replicated, may hold values from -6 to 6
- w_grid_self: bfloat16 [512, 512], replicated, may hold values from -0.25 to 0.25
- w_grid_agg: bfloat16 [512, 512], replicated, may hold values from -0.1875 to 0.1875
- w_grid_out: bfloat16 [512, 227], replicated, may hold values from -0.25 to 0.25
Outputs:
- pred: bfloat16 [65536, 227], P(('lat', 'lon'))
The draws below stay inside these ranges and needn't reach their ends.
Inputs may be any that keep to these rules, and one draw needn't show every extreme that they name: `enc_dest`: patch p lies at patch row p // 8 and column p % 8; cell c lies on the device of index c // 2048 (lat index times 8 plus lon index). The first entry of a row is the cell's own patch. The second is a different patch whose row differs by at most one (no wrap) and whose column differs by at most one, columns wrapping around. Among the cells of one device, no patch is named in the second entry by more than 512 cells, and some patch by exactly 512. `mesh_src`: node n lies in patch n // 512. Every sender lies in the receiver's patch or in one whose row differs by at most one (no wrap) and whose column differs by at most one, columns wrapping around.
All inputs are finite; a program needn't handle non-finite values.
Results may differ from the reference program's by a relative error of at most 0.014.
Values may be sent and summed in bfloat16 or wider, within the bound.
No kernel may reach another device: no remote copies, remote signals or barrier semaphores. Data moves between devices by JAX's collectives and lax.ppermute only.
A program may use at most 128 MiB of HBM per device.

```python
import math
import jax
import jax.numpy as jnp

LATENT = 512
VARS = 227
GRID_DEV = 2048
MESH_DEV = 512
DEG = 8
GRID = 65536
MESH = 16384
CAP = 512
N_LAT = 4
N_LON = 8
DEVICES = 32


def draw_mesh_src(key, part):
    first, second, third = jax.random.split(key, 3)
    index = jnp.arange(MESH, dtype=jnp.int32)
    patch = index // MESH_DEV
    row = patch // N_LON
    column = patch % N_LON
    shift_row = jax.random.randint(first, (MESH, DEG), -1, 2, dtype=jnp.int32)
    shift_col = jax.random.randint(second, (MESH, DEG), -1, 2, dtype=jnp.int32)
    node = jax.random.randint(third, (MESH, DEG), 0, MESH_DEV, dtype=jnp.int32)
    new_row = jnp.clip(row[:, None] + shift_row, 0, N_LAT - 1)
    new_col = (column[:, None] + shift_col) % N_LON
    return ((new_row * N_LON + new_col) * MESH_DEV + node).astype(jnp.int32)


def draw_enc_dest(key, part):
    first, second = jax.random.split(jax.random.fold_in(key, 71), 2)
    device = jnp.arange(DEVICES, dtype=jnp.int32)
    row = device // N_LON
    column = device % N_LON
    step_rows = jnp.array([-1, -1, -1, 0, 0, 1, 1, 1], dtype=jnp.int32)
    step_cols = jnp.array([-1, 0, 1, -1, 1, -1, 0, 1], dtype=jnp.int32)
    moved = row[:, None] + step_rows[None, :]
    valid = (moved >= 0) & (moved < N_LAT)
    score = jnp.where(valid, 0, 8).astype(jnp.int32) + jnp.arange(8, dtype=jnp.int32)[None, :]
    order = jnp.argsort(score, axis=1).astype(jnp.int32)
    count = jnp.sum(valid.astype(jnp.int32), axis=1)
    busy = jax.random.randint(first, (DEVICES,), 0, count, dtype=jnp.int32)
    keys = jax.random.split(second, DEVICES)
    perms = jax.vmap(lambda k: jax.random.permutation(k, GRID_DEV))(keys).astype(jnp.int32)
    ranks = jnp.argsort(perms, axis=1).astype(jnp.int32)
    others = (busy[:, None] + 1 + (ranks - CAP) % (count[:, None] - 1)) % count[:, None]
    pick = jnp.where(ranks < CAP, busy[:, None], others).astype(jnp.int32)
    direction = jnp.take_along_axis(order, pick, axis=1)
    new_row = row[:, None] + step_rows[direction]
    new_col = (column[:, None] + step_cols[direction]) % N_LON
    second_patch = (new_row * N_LON + new_col).astype(jnp.int32)
    first_patch = jnp.broadcast_to(device[:, None], (DEVICES, GRID_DEV)).astype(jnp.int32)
    both = jnp.stack([first_patch, second_patch], axis=-1)
    return both.reshape(GRID, 2).astype(jnp.int32)


def place_ends(values, rng, least, top_value):
    dims = values.shape
    spot = [jax.random.randint(jax.random.fold_in(rng, axis), (), 0, dims[axis]) for axis in range(len(dims))]
    values = values.at[tuple(spot)].set(least)
    longest = dims.index(max(dims))
    spot[longest] = (spot[longest] + 1) % dims[longest]
    return values.at[tuple(spot)].set(top_value)


def level_of(key, extent, cuts, least, top_value):
    factor_of = 1.0
    for dim, parts in cuts:
        heights = jax.random.uniform(jax.random.fold_in(jax.random.fold_in(key, 6), dim), (parts,), jnp.float32, least / len(cuts), top_value / len(cuts))
        factor_of = factor_of * jnp.repeat(jnp.exp(heights), extent[dim] // parts).reshape((-1,) + (1,) * (len(extent) - 1 - dim))
    return factor_of


def centred(key, dims, width, bound, shards=(), kind=jnp.bfloat16):
    result = width * jax.random.normal(key, dims, jnp.float32)
    if shards:
        result = result * level_of(key, dims, shards, -0.22, 0.18)
    return jnp.clip(result, -bound, bound).astype(kind)


def setup_inputs(seed: int = 0) -> dict:
    seeds = jax.random.split(jax.random.key(seed), 25)
    grid_in = centred(seeds[0], (GRID, VARS), 1.0, 6.0, ((0, 32),))
    mesh_emb = centred(seeds[1], (MESH, LATENT), 1.0, 6.0, ((0, 32),))
    enc_dest = draw_enc_dest(jax.random.fold_in(seeds[24], 71), 0)
    enc_node = place_ends(jax.random.randint(seeds[3], (GRID, 2), 0, MESH_DEV), jax.random.fold_in(seeds[3], 1), 0, MESH_DEV - 1).astype(jnp.int32)
    enc_dist = jnp.clip(jnp.exp(math.log(2.0) - 2.3025851 * jax.random.uniform(seeds[4], (GRID, 2), jnp.float32) ** level_of(seeds[4], (GRID, 2), ((0, 32),), -0.2, 0.2)), 0.2, 2.0)
    dec_dist = jnp.clip(jnp.exp(math.log(2.0) - 2.3025851 * jax.random.uniform(seeds[5], (GRID, 2), jnp.float32) ** level_of(seeds[5], (GRID, 2), ((0, 32),), -0.2, 0.2)), 0.2, 2.0)
    mesh_src = draw_mesh_src(jax.random.fold_in(seeds[24], 71), 0)
    proc_dist = jnp.clip(jnp.exp(math.log(2.0) - 2.3025851 * jax.random.uniform(seeds[7], (MESH, DEG), jnp.float32) ** level_of(seeds[7], (MESH, DEG), ((0, 32),), -0.2, 0.2)), 0.2, 2.0)
    w_grid_in = centred(seeds[8], (VARS, LATENT), VARS ** -0.5, 0.375)
    w_enc_src = centred(seeds[9], (LATENT, LATENT), LATENT ** -0.5, 0.25)
    w_enc_dist = centred(seeds[10], (LATENT,), 1.0, 6.0, (), jnp.float32)
    w_mesh_self = centred(seeds[11], (LATENT, LATENT), LATENT ** -0.5, 0.25)
    w_mesh_agg = centred(seeds[12], (LATENT, LATENT), (8 * LATENT) ** -0.5, 0.09375)
    w_proc_send = centred(seeds[13], (LATENT, LATENT), LATENT ** -0.5, 0.25)
    w_proc_recv = centred(seeds[14], (LATENT, LATENT), LATENT ** -0.5, 0.25)
    w_proc_dist = centred(seeds[15], (LATENT,), 1.0, 6.0, (), jnp.float32)
    w_proc_self = centred(seeds[16], (LATENT, LATENT), LATENT ** -0.5, 0.25)
    w_proc_agg = centred(seeds[17], (LATENT, LATENT), (4 * LATENT) ** -0.5, 0.125)
    w_dec_send = centred(seeds[18], (LATENT, LATENT), LATENT ** -0.5, 0.25)
    w_dec_recv = centred(seeds[19], (LATENT, LATENT), LATENT ** -0.5, 0.25)
    w_dec_dist = centred(seeds[20], (LATENT,), 1.0, 6.0, (), jnp.float32)
    w_grid_self = centred(seeds[21], (LATENT, LATENT), LATENT ** -0.5, 0.25)
    w_grid_agg = centred(seeds[22], (LATENT, LATENT), (2 * LATENT) ** -0.5, 0.1875)
    w_grid_out = centred(seeds[23], (LATENT, VARS), LATENT ** -0.5, 0.25)
    return dict(grid_in=grid_in, mesh_emb=mesh_emb, enc_dest=enc_dest, enc_node=enc_node, enc_dist=enc_dist, dec_dist=dec_dist, mesh_src=mesh_src, proc_dist=proc_dist, w_grid_in=w_grid_in, w_enc_src=w_enc_src, w_enc_dist=w_enc_dist, w_mesh_self=w_mesh_self, w_mesh_agg=w_mesh_agg, w_proc_send=w_proc_send, w_proc_recv=w_proc_recv, w_proc_dist=w_proc_dist, w_proc_self=w_proc_self, w_proc_agg=w_proc_agg, w_dec_send=w_dec_send, w_dec_recv=w_dec_recv, w_dec_dist=w_dec_dist, w_grid_self=w_grid_self, w_grid_agg=w_grid_agg, w_grid_out=w_grid_out)


def reference(grid_in, mesh_emb, enc_dest, enc_node, enc_dist, dec_dist, mesh_src, proc_dist, w_grid_in, w_enc_src, w_enc_dist, w_mesh_self, w_mesh_agg, w_proc_send, w_proc_recv, w_proc_dist, w_proc_self, w_proc_agg, w_dec_send, w_dec_recv, w_dec_dist, w_grid_self, w_grid_agg, w_grid_out):
    grid_h = jax.nn.silu(jnp.dot(grid_in, w_grid_in, preferred_element_type=jnp.float32)).astype(jnp.bfloat16)
    enc_proj = jnp.dot(grid_h, w_enc_src, preferred_element_type=jnp.float32)
    enc_msg = jax.nn.silu(enc_proj[:, None, :] + enc_dist[:, :, None] * w_enc_dist).astype(jnp.bfloat16)
    target = (enc_dest * MESH_DEV + enc_node).astype(jnp.int32).reshape(-1)
    enc_agg = jax.ops.segment_sum(enc_msg.reshape(-1, LATENT).astype(jnp.float32), target, num_segments=MESH).astype(jnp.bfloat16)
    mesh_upd = jnp.dot(mesh_emb, w_mesh_self, preferred_element_type=jnp.float32) + jnp.dot(enc_agg, w_mesh_agg, preferred_element_type=jnp.float32)
    mesh_h = (mesh_emb.astype(jnp.float32) + jax.nn.silu(mesh_upd)).astype(jnp.bfloat16)
    proc_send = jnp.dot(mesh_h, w_proc_send, preferred_element_type=jnp.float32).astype(jnp.bfloat16)
    proc_recv = jnp.dot(mesh_h, w_proc_recv, preferred_element_type=jnp.float32)
    gathered = jnp.take(proc_send, mesh_src.reshape(-1), axis=0).reshape(MESH, DEG, LATENT).astype(jnp.float32)
    proc_msg = jax.nn.silu(gathered + proc_recv[:, None, :] + proc_dist[:, :, None] * w_proc_dist)
    proc_agg = jnp.sum(proc_msg, axis=1).astype(jnp.bfloat16)
    proc_upd = jnp.dot(mesh_h, w_proc_self, preferred_element_type=jnp.float32) + jnp.dot(proc_agg, w_proc_agg, preferred_element_type=jnp.float32)
    mesh_out = (mesh_h.astype(jnp.float32) + jax.nn.silu(proc_upd)).astype(jnp.bfloat16)
    dec_send = jnp.dot(mesh_out, w_dec_send, preferred_element_type=jnp.float32).astype(jnp.bfloat16)
    dec_recv = jnp.dot(grid_h, w_dec_recv, preferred_element_type=jnp.float32)
    fetched = jnp.take(dec_send, target, axis=0).reshape(GRID, 2, LATENT).astype(jnp.float32)
    dec_msg = jax.nn.silu(fetched + dec_recv[:, None, :] + dec_dist[:, :, None] * w_dec_dist)
    dec_agg = jnp.sum(dec_msg, axis=1).astype(jnp.bfloat16)
    grid_upd = jnp.dot(grid_h, w_grid_self, preferred_element_type=jnp.float32) + jnp.dot(dec_agg, w_grid_agg, preferred_element_type=jnp.float32)
    grid_z = jax.nn.silu(grid_upd).astype(jnp.bfloat16)
    pred = grid_in.astype(jnp.float32) + jnp.dot(grid_z, w_grid_out, preferred_element_type=jnp.float32)
    return pred.astype(jnp.bfloat16)
```

```python
import functools

import jax
import jax.numpy as jnp
from jax import lax
from jax.experimental import pallas as pl
from jax.experimental.pallas import tpu as pltpu
from jax.sharding import PartitionSpec as P

F32, BF16 = jnp.float32, jnp.bfloat16
LANE = 128
VM = pl.BlockSpec(memory_space=pltpu.VMEM)
SM = pl.BlockSpec(memory_space=pltpu.SMEM)


def mm(a, b):
    return jnp.dot(a, b, preferred_element_type=F32)


def gate(half):
    return half * jnp.tanh(half) + half


def across_pair(block):
    n = lax.axis_size("lat")
    return lax.ppermute(block, "lat", [(i, i ^ 1) for i in range(n)])


def across_band(block):
    n = lax.axis_size("lat")
    pairs = []
    for i in range(1, n - 1, 2):
        pairs += [(i, i + 1), (i + 1, i)]
    return lax.ppermute(block, "lat", pairs)


def across_columns(block):
    n = lax.axis_size("lon")
    return lax.ppermute(block, "lon", [(i, i ^ 1) for i in range(n)])


def two_columns(block, sign):
    n = lax.axis_size("lon")
    pairs = [(i, (i + (2 * sign if i % 2 == 0 else -2 * sign)) % n) for i in range(n)]
    return lax.ppermute(block, "lon", pairs)


def slot_of(patch, n_lon, my_lat, my_lon):
    row, col = patch // n_lon, patch % n_lon
    row_slot = jnp.where(row == my_lat, 0, jnp.where(row == (my_lat ^ 1), 1, 2))
    col_slot = jnp.where(col == my_lon, 0, jnp.where(col == (my_lon ^ 1), 1, 2))
    return col_slot * 3 + row_slot


def halo(own):
    pair_col = across_columns(own)
    own_band = across_band(own)
    far_col = two_columns(pair_col, 1)
    own_pair = across_pair(own)
    pc_pair = across_pair(pair_col)
    pc_band = across_band(pair_col)
    fc_pair = across_pair(far_col)
    fc_band = across_band(far_col)
    return [own, own_pair, own_band, pair_col, pc_pair, pc_band, far_col, fc_pair, fc_band]


def fill(tab, base, block, lanes, scale, step=64):
    rows = block.shape[0]

    def go(i, carry):
        r = pl.multiple_of(i * step, step)
        for k in range(lanes):
            piece = block[pl.ds(r, step), k * LANE : (k + 1) * LANE].astype(F32)
            if scale != 1:
                piece = piece * scale
            tab[pl.ds(base + r * lanes + k, step, stride=lanes), :] = piece
        return carry

    lax.fori_loop(0, rows // step, go, 0)


def mesh_kernel(emb, own, pair, band, cols, w_self, w_agg, w_send, mesh_h, send):
    agg = (own[...] + pair[...].astype(F32) + band[...].astype(F32) + cols[...].astype(F32)).astype(BF16)
    upd = mm(emb[...], w_self[...]) + mm(agg, w_agg[...])
    h = (emb[...].astype(F32) + gate(0.5 * upd)).astype(BF16)
    mesh_h[...] = h
    send[...] = mm(h, w_send[...]).astype(BF16)


def mesh_call(emb, own, pair, band, cols, w_self, w_agg, w_send):
    shape = jax.ShapeDtypeStruct(emb.shape, BF16)
    rows, width = emb.shape
    return pl.pallas_call(
        mesh_kernel,
        out_shape=(shape, shape),
        in_specs=[VM] * 8,
        out_specs=(VM, VM),
        compiler_params=pltpu.CompilerParams(vmem_limit_bytes=32 * 2**20),
        cost_estimate=pl.CostEstimate(
            flops=6 * rows * width * width, bytes_accessed=12 * rows * width, transcendentals=rows * width
        ),
    )(emb, own, pair, band, cols, w_self, w_agg, w_send)


def recv_kernel(mesh_h, w_recv, recv8):
    rows, width = mesh_h.shape
    lanes = width // LANE
    half = 0.5 * mm(mesh_h[...], w_recv[...])
    for k in range(lanes):
        piece = half[:, k * LANE : (k + 1) * LANE]
        recv8[pl.ds(k, rows, stride=2 * lanes), :] = piece
        recv8[pl.ds(k + lanes, rows, stride=2 * lanes), :] = piece


def recv_call(mesh_h, w_recv):
    rows, width = mesh_h.shape
    return pl.pallas_call(
        recv_kernel,
        out_shape=jax.ShapeDtypeStruct((rows * 2 * width // LANE, LANE), F32),
        in_specs=[VM, VM],
        out_specs=VM,
        compiler_params=pltpu.CompilerParams(vmem_limit_bytes=32 * 2**20),
        cost_estimate=pl.CostEstimate(
            flops=2 * rows * width * width, bytes_accessed=12 * rows * width, transcendentals=0
        ),
    )(mesh_h, w_recv)


def proc_kernel(idx, dist, w8, recv8, *refs, unroll):
    blocks, (mesh_h, w_self, w_agg, w_send, out, tab, acc) = refs[:9], refs[9:]
    rows, width = out.shape
    lanes = width // LANE
    degree = idx.shape[0] // rows
    for s, b in enumerate(blocks):
        fill(tab, lanes * (1 + s * rows), b, lanes, 0.5)
    top = lax.broadcasted_iota(jnp.int32, (2 * lanes, LANE), 0) < lanes
    wd = w8[...]

    def node(n):
        at = pl.ds(pl.multiple_of(n * 2 * lanes, 2 * lanes), 2 * lanes)
        recv = recv8[at, :]
        total = None
        for j in range(0, degree, 2):
            e = n * degree + j
            first = tab[pl.ds(idx[e] + lanes, 2 * lanes), :]
            second = tab[pl.ds(idx[e + 1], 2 * lanes), :]
            both = jnp.where(top, first, second)
            far = jnp.where(top, dist[e], dist[e + 1])
            msg = gate(both + (recv + far * wd))
            total = msg if total is None else total + msg
        acc[at, :] = total

    def some(i, carry):
        for u in range(unroll):
            node(i * unroll + u)
        return carry

    lax.fori_loop(0, rows // unroll, some, 0)
    upd = mm(mesh_h[...], w_self[...])
    for k in range(lanes):
        agg = acc[pl.ds(k, rows, stride=2 * lanes), :] + acc[pl.ds(k + lanes, rows, stride=2 * lanes), :]
        upd += mm(agg.astype(BF16), w_agg[k * LANE : (k + 1) * LANE, :])
    mesh_out = (mesh_h[...].astype(F32) + gate(0.5 * upd)).astype(BF16)
    out[...] = mm(mesh_out, w_send[...]).astype(BF16)


def proc_call(idx, dist, w8, recv8, blocks, mesh_h, w_self, w_agg, w_send):
    rows, width = mesh_h.shape
    lanes = width // LANE
    return pl.pallas_call(
        functools.partial(proc_kernel, unroll=8),
        out_shape=jax.ShapeDtypeStruct((rows, width), BF16),
        in_specs=[SM, SM] + [VM] * 15,
        out_specs=VM,
        scratch_shapes=[
            pltpu.VMEM((lanes * (9 * rows + 2), LANE), F32),
            pltpu.VMEM((rows * 2 * lanes, LANE), F32),
        ],
        compiler_params=pltpu.CompilerParams(vmem_limit_bytes=40 * 2**20),
        cost_estimate=pl.CostEstimate(
            flops=6 * rows * width * width, bytes_accessed=32 * rows * width, transcendentals=idx.shape[0] * width
        ),
    )(idx, dist, w8, recv8, *blocks, mesh_h, w_self, w_agg, w_send)


def cell_kernel(grid_h, w_recv, w_self, recv, upd):
    rows, width = grid_h.shape
    lanes = width // LANE
    half = 0.5 * mm(grid_h[...], w_recv[...])
    for k in range(lanes):
        recv[pl.ds(k, rows, stride=lanes), :] = half[:, k * LANE : (k + 1) * LANE]
    upd[...] = mm(grid_h[...], w_self[...])


def cell_call(grid_h, w_recv, w_self, step=256):
    rows, width = grid_h.shape
    lanes = width // LANE
    return pl.pallas_call(
        cell_kernel,
        grid=(rows // step,),
        out_shape=(jax.ShapeDtypeStruct((rows * lanes, LANE), F32), jax.ShapeDtypeStruct((rows, width), F32)),
        in_specs=[pl.BlockSpec((step, width), lambda i: (i, 0)), VM, VM],
        out_specs=(
            pl.BlockSpec((step * lanes, LANE), lambda i: (i, 0)),
            pl.BlockSpec((step, width), lambda i: (i, 0)),
        ),
        compiler_params=pltpu.CompilerParams(vmem_limit_bytes=32 * 2**20),
        cost_estimate=pl.CostEstimate(
            flops=4 * rows * width * width, bytes_accessed=10 * rows * width, transcendentals=0
        ),
    )(grid_h, w_recv, w_self)


def edge_messages(idx, dist, start, tab, recv, put, wd, cells, lanes, unroll):
    top = lax.broadcasted_iota(jnp.int32, (2 * lanes, LANE), 0) < lanes

    def pair(c):
        at = pl.ds(pl.multiple_of(c * lanes, 2 * lanes), 2 * lanes)
        first = tab[pl.ds(idx[start + c] + lanes, 2 * lanes), :]
        second = tab[pl.ds(idx[start + c + 1], 2 * lanes), :]
        far = jnp.where(top, dist[start + c], dist[start + c + 1])
        put(at, gate(jnp.where(top, first, second) + (recv[at, :] + far * wd)))

    def some(i, carry):
        for u in range(unroll):
            pair((i * unroll + u) * 2)
        return carry

    lax.fori_loop(0, cells // (2 * unroll), some, 0)


def near_kernel(idx, dist, w8, recv, own, msg, tab, *, unroll):
    lanes = own.shape[1] // LANE
    step = recv.shape[0] // lanes
    i = pl.program_id(0)

    @pl.when(i == 0)
    def _():
        fill(tab, lanes, own, lanes, 0.5)

    def put(at, value):
        msg[at, :] = value

    edge_messages(idx, dist, i * step, tab, recv, put, w8[...], step, lanes, unroll)


def near_call(idx, dist, w8, recv, own, step=512):
    rows, width = own.shape
    cells = idx.shape[0]
    lanes = width // LANE
    cut = pl.BlockSpec((step * lanes, LANE), lambda i: (i, 0))
    return pl.pallas_call(
        functools.partial(near_kernel, unroll=16),
        grid=(cells // step,),
        out_shape=jax.ShapeDtypeStruct((cells * lanes, LANE), F32),
        in_specs=[SM, SM, VM, cut, VM],
        out_specs=cut,
        scratch_shapes=[pltpu.VMEM((lanes * (rows + 2), LANE), F32)],
        compiler_params=pltpu.CompilerParams(vmem_limit_bytes=32 * 2**20),
        cost_estimate=pl.CostEstimate(
            flops=8 * cells * width, bytes_accessed=8 * cells * width, transcendentals=cells * width
        ),
    )(idx, dist, w8, recv, own)


def far_kernel(idx, dist, w8, recv, near, upd, grid_in, *refs, unroll):
    blocks, (w_agg, w_out, out, tab, acc) = refs[:8], refs[8:]
    rows, width = blocks[0].shape
    lanes = width // LANE
    step = out.shape[0]
    i = pl.program_id(0)

    @pl.when(i == 0)
    def _():
        for s, b in enumerate(blocks):
            fill(tab, lanes * (1 + s * rows), b, lanes, 0.5)

    def put(at, value):
        acc[at, :] = value + near[at, :]

    edge_messages(idx, dist, i * step, tab, recv, put, w8[...], step, lanes, unroll)
    total = upd[...]
    for k in range(lanes):
        agg = acc[pl.ds(k, step, stride=lanes), :].astype(BF16)
        total += mm(agg, w_agg[k * LANE : (k + 1) * LANE, :])
    z = gate(0.5 * total).astype(BF16)
    out[...] = (grid_in[...].astype(F32) + mm(z, w_out[...])).astype(BF16)


def far_call(idx, dist, w8, recv, near, upd, grid_in, blocks, w_agg, w_out, step=256):
    cells, width = upd.shape
    rows = blocks[0].shape[0]
    lanes = width // LANE
    n_vars = grid_in.shape[1]
    cut = pl.BlockSpec((step * lanes, LANE), lambda i: (i, 0))
    flat = pl.BlockSpec((step, width), lambda i: (i, 0))
    some = pl.BlockSpec((step, n_vars), lambda i: (i, 0))
    return pl.pallas_call(
        functools.partial(far_kernel, unroll=16),
        grid=(cells // step,),
        out_shape=jax.ShapeDtypeStruct(grid_in.shape, BF16),
        in_specs=[SM, SM, VM, cut, cut, flat, some] + [VM] * 10,
        out_specs=some,
        scratch_shapes=[
            pltpu.VMEM((lanes * (8 * rows + 2), LANE), F32),
            pltpu.VMEM((step * lanes, LANE), F32),
        ],
        compiler_params=pltpu.CompilerParams(vmem_limit_bytes=40 * 2**20),
        cost_estimate=pl.CostEstimate(
            flops=4 * cells * width * width, bytes_accessed=16 * cells * width, transcendentals=2 * cells * width
        ),
    )(idx, dist, w8, recv, near, upd, grid_in, *blocks, w_agg, w_out)


def doubled(w_dist):
    return jnp.tile((0.5 * w_dist).reshape(-1, LANE), (2, 1))


def shards(
    grid_in,
    mesh_emb,
    enc_dest,
    enc_node,
    enc_dist,
    dec_dist,
    mesh_src,
    proc_dist,
    w_grid_in,
    w_enc_src,
    w_enc_dist,
    w_mesh_self,
    w_mesh_agg,
    w_proc_send,
    w_proc_recv,
    w_proc_dist,
    w_proc_self,
    w_proc_agg,
    w_dec_send,
    w_dec_recv,
    w_dec_dist,
    w_grid_self,
    w_grid_agg,
    w_grid_out,
):
    n_lon = lax.axis_size("lon")
    width = w_grid_in.shape[1]
    lanes = width // LANE
    rows = mesh_emb.shape[0]
    where = (n_lon, lax.axis_index("lat"), lax.axis_index("lon"))

    grid_h = gate(0.5 * mm(grid_in, w_grid_in)).astype(BF16)
    enc_proj = mm(grid_h, w_enc_src)
    msg0 = gate(0.5 * (enc_proj + enc_dist[:, 0:1] * w_enc_dist)).astype(BF16)
    msg1 = gate(0.5 * (enc_proj + enc_dist[:, 1:2] * w_enc_dist)).astype(BF16)
    far_slot = slot_of(enc_dest[:, 1], *where)
    far_key = far_slot * rows + enc_node[:, 1]

    def partial(first, count):
        ids = first * rows + jnp.arange(count * rows, dtype=jnp.int32)
        select = (far_key[None, :] == ids[:, None]).astype(BF16)
        return mm(select, msg1).astype(BF16)

    part_z = partial(6, 3)
    z_pair = across_pair(part_z[rows : 2 * rows])
    z_band = across_band(part_z[2 * rows :])
    part_p = partial(3, 3)
    p_pair = across_pair(part_p[rows : 2 * rows])
    p_band = across_band(part_p[2 * rows :])
    part_o = partial(1, 2)
    o_pair = across_pair(part_o[:rows])
    o_band = across_band(part_o[rows:])
    own_select = (enc_node[:, 0][None, :] == jnp.arange(rows, dtype=jnp.int32)[:, None]).astype(BF16)
    own = mm(own_select, msg0)
    z_sum = (part_z[:rows].astype(F32) + z_pair.astype(F32) + z_band.astype(F32)).astype(BF16)
    z_in = two_columns(z_sum, -1)
    p_sum = (part_p[:rows].astype(F32) + p_pair.astype(F32) + p_band.astype(F32) + z_in.astype(F32)).astype(BF16)
    p_in = across_columns(p_sum)
    mesh_h, proc_send = mesh_call(mesh_emb, own, o_pair, o_band, p_in, w_mesh_self, w_mesh_agg, w_proc_send)

    proc_idx = ((slot_of(mesh_src // rows, *where) * rows + mesh_src % rows) * lanes).reshape(-1)
    nearby = halo(proc_send)
    recv8 = recv_call(mesh_h, w_proc_recv)
    dec_send = proc_call(
        proc_idx,
        proc_dist.reshape(-1),
        doubled(w_proc_dist),
        recv8,
        nearby,
        mesh_h,
        w_proc_self,
        w_proc_agg,
        w_dec_send,
    )

    dec_recv, grid_upd = cell_call(grid_h, w_dec_recv, w_grid_self)
    around = halo(dec_send)
    w8 = doubled(w_dec_dist)
    near = near_call(enc_node[:, 0] * lanes, dec_dist[:, 0], w8, dec_recv, dec_send)
    return far_call(
        (far_key - rows) * lanes,
        dec_dist[:, 1],
        w8,
        dec_recv,
        near,
        grid_upd,
        grid_in,
        around[1:],
        w_grid_agg,
        w_grid_out,
    )


def solution(mesh):
    split = P(("lat", "lon"), None)
    in_specs = (split,) * 8 + (P(),) * 16
    return jax.shard_map(shards, mesh=mesh, in_specs=in_specs, out_specs=split, check_vma=False)
```

```python
import functools

import jax
import jax.numpy as jnp
from jax import lax
from jax.experimental import pallas as pl
from jax.experimental.pallas import tpu as pltpu
from jax.sharding import PartitionSpec as P

F32, BF16 = jnp.float32, jnp.bfloat16
LANE = 128
VM = pl.BlockSpec(memory_space=pltpu.VMEM)
SM = pl.BlockSpec(memory_space=pltpu.SMEM)


def mm(a, b):
    return jnp.dot(a, b, preferred_element_type=F32)


def gate(half):
    return half * jnp.tanh(half) + half


def across_pair(block):
    n = lax.axis_size("lat")
    return lax.ppermute(block, "lat", [(i, i ^ 1) for i in range(n)])


def across_band(block):
    n = lax.axis_size("lat")
    pairs = []
    for i in range(1, n - 1, 2):
        pairs += [(i, i + 1), (i + 1, i)]
    return lax.ppermute(block, "lat", pairs)


def across_columns(block):
    n = lax.axis_size("lon")
    return lax.ppermute(block, "lon", [(i, i ^ 1) for i in range(n)])


def across_corner(block):
    rows, n = lax.axis_size("lat"), lax.axis_size("lon")
    pairs = []
    for r in range(1, rows - 1, 2):
        for c in range(n):
            here, there = r * n + c, (r + 1) * n + (c + (1 if c % 2 else -1)) % n
            pairs += [(here, there), (there, here)]
    return lax.ppermute(block, ("lat", "lon"), pairs)


def two_columns(block, sign):
    n = lax.axis_size("lon")
    pairs = [(i, (i + (2 * sign if i % 2 == 0 else -2 * sign)) % n) for i in range(n)]
    return lax.ppermute(block, "lon", pairs)


def slot_of(patch, n_lon, my_lat, my_lon):
    row, col = patch // n_lon, patch % n_lon
    row_slot = jnp.where(row == my_lat, 0, jnp.where(row == (my_lat ^ 1), 1, 2))
    col_slot = jnp.where(col == my_lon, 0, jnp.where(col == (my_lon ^ 1), 1, 2))
    return col_slot * 3 + row_slot


def halo(own, pair_col):
    own_band = across_band(own)
    far_col = two_columns(pair_col, 1)
    own_pair = across_pair(own)
    pc_pair = across_pair(pair_col)
    pc_band = across_band(pair_col)
    fc_pair = across_pair(far_col)
    fc_band = across_band(far_col)
    return [own, own_pair, own_band, pair_col, pc_pair, pc_band, far_col, fc_pair, fc_band]


def params(mib):
    return pltpu.CompilerParams(vmem_limit_bytes=mib * 2**20)


def cost(flops, moved, exps=0):
    return pl.CostEstimate(flops=flops, bytes_accessed=moved, transcendentals=exps)


def grouped(full, spread, rows, lanes, every, first=0):
    for k in range(lanes):
        spread[pl.ds(first + k, rows, stride=every), :] = full[:, k * LANE : (k + 1) * LANE]


def widen(tab, base, block, step=256):
    def go(i, carry):
        r = pl.multiple_of(i * step, step)
        tab[pl.ds(base + r, step), :] = block[pl.ds(r, step), :].astype(F32)
        return carry

    lax.fori_loop(0, block.shape[0] // step, go, 0)


def edge_kernel(cells_in, key, dist, w_in, w_src, wd, grid_h, msg0, msg1, own, pair, band, *, first, step):
    cells, width = grid_h.shape
    rows = own.shape[0]
    lengths = dist[...].T
    for c in range(0, cells, step):
        cut = slice(c, c + step)
        half = 0.5 * lax.dot_general(
            cells_in[:, cut], w_in[...], (((0,), (0,)), ((), ())), preferred_element_type=F32
        )
        h = gate(half).astype(BF16)
        grid_h[cut, :] = h
        proj = 0.5 * mm(h, w_src[...])
        msg0[cut, :] = gate(proj + lengths[cut, 0:1] * wd[...]).astype(BF16)
        msg1[cut, :] = gate(proj + lengths[cut, 1:2] * wd[...]).astype(BF16)
    for s, out in enumerate((own, pair, band)):
        ids = (first + s) * rows + lax.broadcasted_iota(jnp.int32, (rows, cells), 0)
        out[...] = mm((key[...] == ids).astype(BF16), msg1[...]).astype(BF16)


def edge_call(cells_in, key, dist, w_in, w_src, wd, rows, first, step=256):
    n_vars, cells = cells_in.shape
    width = w_in.shape[1]
    tall = jax.ShapeDtypeStruct((cells, width), BF16)
    patch = jax.ShapeDtypeStruct((rows, width), BF16)
    return pl.pallas_call(
        functools.partial(edge_kernel, first=first, step=step),
        out_shape=(tall,) * 3 + (patch,) * 3,
        in_specs=[VM] * 6,
        out_specs=(VM,) * 6,
        compiler_params=params(16),
        cost_estimate=cost(8 * rows * cells * width, 12 * cells * width, 3 * cells * width),
    )(cells_in, key, dist, w_in, w_src, wd)


def mesh_kernel(emb, own, s0, s1, s2, s3, w_self, w_agg, w_send, mesh_h, send, spread):
    rows, width = emb.shape
    agg = own[...]
    for part in (s0, s1, s2, s3):
        agg += part[...].astype(F32)
    agg = agg.astype(BF16)
    upd = mm(emb[...], w_self[...]) + mm(agg, w_agg[...])
    h = (emb[...].astype(F32) + gate(0.5 * upd)).astype(BF16)
    mesh_h[...] = h
    grouped(0.5 * mm(h, w_send[...]), spread, rows, width // LANE, width // LANE)
    send[...] = spread[...].astype(BF16)


def mesh_call(emb, own, sums, w_self, w_agg, w_send):
    rows, width = emb.shape
    flat = (rows * width // LANE, LANE)
    return pl.pallas_call(
        mesh_kernel,
        out_shape=(jax.ShapeDtypeStruct((rows, width), BF16), jax.ShapeDtypeStruct(flat, BF16)),
        in_specs=[VM] * 9,
        out_specs=(VM, VM),
        scratch_shapes=[pltpu.VMEM(flat, F32)],
        compiler_params=params(8),
        cost_estimate=cost(6 * rows * width * width, 16 * rows * width, rows * width),
    )(emb, own, *sums, w_self, w_agg, w_send)


def recv_kernel(mesh_h, dist, w_recv, w_self, wd, recv, upd):
    rows, width = mesh_h.shape
    lanes = width // LANE
    degree = dist.shape[0]
    half = 0.5 * mm(mesh_h[...], w_recv[...])
    lengths = dist[...].T
    for j in range(degree):
        grouped(half + lengths[:, j : j + 1] * wd[...], recv, rows, lanes, degree * lanes, j * lanes)
    upd[...] = mm(mesh_h[...], w_self[...])


def recv_call(mesh_h, dist, w_recv, w_self, wd):
    rows, width = mesh_h.shape
    degree = dist.shape[0]
    return pl.pallas_call(
        recv_kernel,
        out_shape=(
            jax.ShapeDtypeStruct((rows * degree * width // LANE, LANE), F32),
            jax.ShapeDtypeStruct((rows, width), F32),
        ),
        in_specs=[VM] * 5,
        out_specs=(VM, VM),
        compiler_params=params(8),
        cost_estimate=cost(4 * rows * width * width, 40 * rows * width),
    )(mesh_h, dist, w_recv, w_self, wd)


def message_pair(tab, idx, a, b, recv, lanes, top):
    first = tab[pl.ds(idx[a] + 2 * lanes, 2 * lanes), :]
    second = tab[pl.ds(idx[b] + lanes, 2 * lanes), :]
    return gate(jnp.where(top, first, second) + recv)


def proc_kernel(idx, recv, *refs, unroll):
    blocks, (mesh_h, upd, w_agg, w_send, out, tab, acc) = refs[:9], refs[9:]
    rows, width = mesh_h.shape
    lanes = width // LANE
    two = 2 * lanes
    degree = idx.shape[0] // rows
    for s, b in enumerate(blocks):
        widen(tab, lanes * (2 + s * rows), b)
    top = lax.broadcasted_iota(jnp.int32, (two, LANE), 0) < lanes

    def node(n):
        total = None
        for j in range(0, degree, 2):
            add = recv[pl.ds(pl.multiple_of((n * degree + j) * lanes, two), two), :]
            msg = message_pair(tab, idx, j * rows + n, (j + 1) * rows + n, add, lanes, top)
            total = msg if total is None else total + msg
        acc[pl.ds(pl.multiple_of(n * two, two), two), :] = total

    def some(i, carry):
        for u in range(unroll):
            node(i * unroll + u)
        return carry

    lax.fori_loop(0, rows // unroll, some, 0)
    agg = [
        (acc[pl.ds(k, rows, stride=two), :] + acc[pl.ds(k + lanes, rows, stride=two), :]).astype(BF16)
        for k in range(lanes)
    ]
    total = upd[...] + mm(jnp.concatenate(agg, axis=1), w_agg[...])
    mesh_out = (mesh_h[...].astype(F32) + gate(0.5 * total)).astype(BF16)
    spread = acc.at[pl.ds(0, rows * lanes), :]
    grouped(0.5 * mm(mesh_out, w_send[...]), spread, rows, lanes, lanes)
    out[...] = spread[...].astype(BF16)


def proc_call(idx, recv, blocks, mesh_h, upd, w_agg, w_send):
    rows, width = mesh_h.shape
    lanes = width // LANE
    return pl.pallas_call(
        functools.partial(proc_kernel, unroll=16),
        out_shape=jax.ShapeDtypeStruct((rows * lanes, LANE), BF16),
        in_specs=[SM] + [VM] * 14,
        out_specs=VM,
        scratch_shapes=[
            pltpu.VMEM((lanes * (9 * rows + 4), LANE), F32),
            pltpu.VMEM((rows * 2 * lanes, LANE), F32),
        ],
        compiler_params=params(16),
        cost_estimate=cost(4 * rows * width * width, 32 * rows * width, idx.size * width),
    )(idx, recv, *blocks, mesh_h, upd, w_agg, w_send)


def cell_kernel(grid_h, dist, w_recv, w_self, wd, recv0, recv1, upd, *, step):
    cells, width = grid_h.shape
    lanes = width // LANE
    lengths = dist[...].T
    for c in range(0, cells, step):
        cut = slice(c, c + step)
        half = 0.5 * mm(grid_h[cut, :], w_recv[...])
        for k, recv in enumerate((recv0, recv1)):
            grouped(half + lengths[cut, k : k + 1] * wd[...], recv, step, lanes, lanes, c * lanes)
        upd[cut, :] = mm(grid_h[cut, :], w_self[...])


def cell_call(grid_h, dist, w_recv, w_self, wd, step=256):
    cells, width = grid_h.shape
    lanes = width // LANE
    flat = jax.ShapeDtypeStruct((cells * lanes, LANE), F32)
    return pl.pallas_call(
        functools.partial(cell_kernel, step=step),
        out_shape=(flat, flat, jax.ShapeDtypeStruct((cells, width), F32)),
        in_specs=[VM] * 5,
        out_specs=(VM,) * 3,
        compiler_params=params(8),
        cost_estimate=cost(4 * cells * width * width, 14 * cells * width),
    )(grid_h, dist, w_recv, w_self, wd)


def cells_kernel(idx, recv, upd, w_agg, *refs, n_blocks, step, unroll):
    blocks, refs = refs[:n_blocks], refs[n_blocks:]
    tab, acc = refs[-2:]
    cells, width = upd.shape
    lanes = width // LANE
    two = 2 * lanes
    size = blocks[0].shape[0]
    for s, b in enumerate(blocks):
        widen(tab, two + s * size, b)
    top = lax.broadcasted_iota(jnp.int32, (two, LANE), 0) < lanes

    def chunk(i, carry):
        base = pl.multiple_of(i * step, step)

        def some(q, carry):
            for u in range(unroll):
                c = (q * unroll + u) * 2
                add = recv[pl.ds(pl.multiple_of((base + c) * lanes, two), two), :]
                msg = message_pair(tab, idx, base + c, base + c + 1, add, lanes, top)
                acc[pl.ds(pl.multiple_of(c * lanes, two), two), :] = msg
            return carry

        lax.fori_loop(0, step // (2 * unroll), some, 0)
        agg = [acc[pl.ds(k, step, stride=lanes), :].astype(BF16) for k in range(lanes)]
        total = upd[pl.ds(base, step), :] + mm(jnp.concatenate(agg, axis=1), w_agg[...])
        if len(refs) == 3:
            refs[0][pl.ds(base, step), :] = total
            return carry
        cells_in, w_out, out = refs[:3]
        z = gate(0.5 * total).astype(BF16)
        change = lax.dot_general(w_out[...], z, (((1,), (1,)), ((), ())), preferred_element_type=F32)
        cut = pl.ds(base, step)
        out[:, cut] = (cells_in[:, cut].astype(F32) + change).astype(BF16)
        return carry

    lax.fori_loop(0, cells // step, chunk, 0)


def cells_call(idx, recv, upd, w_agg, blocks, last=(), step=512):
    cells, width = upd.shape
    lanes = width // LANE
    shape = jax.ShapeDtypeStruct(last[0].shape, BF16) if last else jax.ShapeDtypeStruct(upd.shape, F32)
    return pl.pallas_call(
        functools.partial(cells_kernel, n_blocks=len(blocks), step=step, unroll=32),
        out_shape=shape,
        in_specs=[SM] + [VM] * (3 + len(blocks) + len(last)),
        out_specs=VM,
        scratch_shapes=[
            pltpu.VMEM((sum(b.shape[0] for b in blocks) + 4 * lanes, LANE), F32),
            pltpu.VMEM((step * lanes, LANE), F32),
        ],
        compiler_params=params(8 + len(blocks) * 2),
        cost_estimate=cost(4 * cells * width * width, 16 * cells * width, 2 * cells * width),
    )(idx, recv, upd, w_agg, *blocks, *last)


def with_done(block, *others):
    return lax.optimization_barrier((block, *others))


def shards(
    grid_in,
    mesh_emb,
    enc_dest,
    enc_node,
    enc_dist,
    dec_dist,
    mesh_src,
    proc_dist,
    w_grid_in,
    w_enc_src,
    w_enc_dist,
    w_mesh_self,
    w_mesh_agg,
    w_proc_send,
    w_proc_recv,
    w_proc_dist,
    w_proc_self,
    w_proc_agg,
    w_dec_send,
    w_dec_recv,
    w_dec_dist,
    w_grid_self,
    w_grid_agg,
    w_grid_out,
):
    width = w_grid_in.shape[1]
    lanes = width // LANE
    rows = mesh_emb.shape[0]
    where = (lax.axis_size("lon"), lax.axis_index("lat"), lax.axis_index("lon"))
    cells_in, dest, node = grid_in.T, enc_dest.T, enc_node.T

    far_key = slot_of(dest[1:], *where) * rows + node[1:]
    grid_h, msg0, msg1, z_own, z_pair, z_band = edge_call(
        cells_in, far_key, enc_dist.T, w_grid_in, w_enc_src, (0.5 * w_enc_dist)[None], rows, 6
    )

    def partial(slot, messages):
        ids = slot * rows + lax.broadcasted_iota(jnp.int32, (rows, 1), 0)
        return mm((far_key == ids).astype(BF16), messages).astype(BF16)

    z_pair, z_band = across_pair(z_pair), across_corner(z_band)
    p_own = partial(3, msg1)
    z_sum = (z_own.astype(F32) + z_pair.astype(F32)).astype(BF16)
    z_sum, msg1 = with_done(z_sum, msg1)
    z_in = two_columns(z_sum, -1)
    p_pair, p_band = across_pair(partial(4, msg1)), across_band(partial(5, msg1))
    p_sum = (p_own.astype(F32) + p_pair.astype(F32) + p_band.astype(F32) + z_in.astype(F32)).astype(BF16)
    own_select = (node[:1] == lax.broadcasted_iota(jnp.int32, (rows, 1), 0)).astype(BF16)
    own = mm(own_select, msg0)
    o_pair, o_band = across_pair(partial(1, msg1)), across_band(partial(2, msg1))
    recv0, recv1, grid_upd = cell_call(grid_h, dec_dist.T, w_dec_recv, w_grid_self, (0.5 * w_dec_dist)[None])
    source = mesh_src.T
    proc_idx = ((slot_of(source // rows, *where) * rows + source % rows) * lanes).reshape(-1)
    near_idx, far_idx = node[0] * lanes, far_key[0] * lanes - rows * lanes
    p_in, own, recv0, recv1, grid_upd, proc_idx, near_idx, far_idx = with_done(
        across_columns(p_sum), own, recv0, recv1, grid_upd, proc_idx, near_idx, far_idx
    )
    mesh_h, proc_send = mesh_call(mesh_emb, own, (o_pair, o_band, p_in, z_band), w_mesh_self, w_mesh_agg, w_proc_send)

    pair_col = across_columns(proc_send)
    recv, mesh_upd = recv_call(mesh_h, proc_dist.T, w_proc_recv, w_proc_self, (0.5 * w_proc_dist)[None])
    pair_col, recv, mesh_upd = with_done(pair_col, recv, mesh_upd)
    nearby = halo(proc_send, pair_col)
    dec_send = proc_call(proc_idx, recv, nearby, mesh_h, mesh_upd, w_proc_agg, w_dec_send)

    pair_col = across_columns(dec_send)
    grid_upd = cells_call(near_idx, recv0, grid_upd, w_grid_agg, [dec_send])
    pair_col, grid_upd = with_done(pair_col, grid_upd)
    around = halo(dec_send, pair_col)[1:]
    pred = cells_call(far_idx, recv1, grid_upd, w_grid_agg, around, (cells_in, w_grid_out.T))
    return pred.T


def solution(mesh):
    split = P(("lat", "lon"), None)
    in_specs = (split,) * 8 + (P(),) * 16
    return jax.shard_map(shards, mesh=mesh, in_specs=in_specs, out_specs=split, check_vma=False)
```

```python
import functools

import jax
import jax.numpy as jnp
from jax import lax
from jax.experimental import pallas as pl
from jax.experimental.pallas import tpu as pltpu
from jax.sharding import PartitionSpec as P

F32, BF16 = jnp.float32, jnp.bfloat16
LANE = 128
VM = pl.BlockSpec(memory_space=pltpu.VMEM)
SM = pl.BlockSpec(memory_space=pltpu.SMEM)
HB = pl.BlockSpec(memory_space=pltpu.HBM)


def mm(a, b):
    return jnp.dot(a, b, preferred_element_type=F32)


def gate(half):
    return half * jnp.tanh(half) + half


def across_pair(block):
    n = lax.axis_size("lat")
    return lax.ppermute(block, "lat", [(i, i ^ 1) for i in range(n)])


def across_band(block):
    n = lax.axis_size("lat")
    pairs = []
    for i in range(1, n - 1, 2):
        pairs += [(i, i + 1), (i + 1, i)]
    return lax.ppermute(block, "lat", pairs)


def across_columns(block):
    n = lax.axis_size("lon")
    return lax.ppermute(block, "lon", [(i, i ^ 1) for i in range(n)])


def two_columns(block, sign):
    n = lax.axis_size("lon")
    pairs = [(i, (i + (2 * sign if i % 2 == 0 else -2 * sign)) % n) for i in range(n)]
    return lax.ppermute(block, "lon", pairs)


def slot_of(patch, n_lon, my_lat, my_lon):
    row, col = patch // n_lon, patch % n_lon
    row_slot = jnp.where(row == my_lat, 0, jnp.where(row == (my_lat ^ 1), 1, 2))
    col_slot = jnp.where(col == my_lon, 0, jnp.where(col == (my_lon ^ 1), 1, 2))
    return col_slot * 3 + row_slot


def halo(own, pair_col):
    own_band = across_band(own)
    far_col = two_columns(pair_col, 1)
    own_pair = across_pair(own)
    pc_pair = across_pair(pair_col)
    pc_band = across_band(pair_col)
    fc_pair = across_pair(far_col)
    fc_band = across_band(far_col)
    return [own, own_pair, own_band, pair_col, pc_pair, pc_band, far_col, fc_pair, fc_band]


def params(mib):
    return pltpu.CompilerParams(vmem_limit_bytes=mib * 2**20)


def cost(flops, moved, exps=0):
    return pl.CostEstimate(flops=flops, bytes_accessed=moved, transcendentals=exps)


def grouped(full, spread, rows, lanes, every, first=0):
    for k in range(lanes):
        spread[pl.ds(first + k, rows, stride=every), :] = full[:, k * LANE : (k + 1) * LANE]


def widen(tab, base, block, step=256):
    def go(i, carry):
        r = pl.multiple_of(i * step, step)
        tab[pl.ds(base + r, step), :] = block[pl.ds(r, step), :].astype(F32)
        return carry

    lax.fori_loop(0, block.shape[0] // step, go, 0)


def around_patch(n_lon):
    row, col = lax.axis_index("lat"), lax.axis_index("lon")
    side = lax.rem(row, 2) * 2 - 1
    turn = lax.rem(col, 2) * 2 - 1
    return [
        r * n_lon + lax.rem(c + n_lon, n_lon)
        for c in (col, col - turn, col + turn)
        for r in (row, row - side, row + side)
    ]


def front_kernel(*refs, n_lon, first, step):
    ins, outs, rest = refs[:7], refs[7:13], refs[13:]
    grid_h, msg1, key, own, pair, band = rest[7:13]
    sems = rest[13]
    copies = [pltpu.make_async_copy(a, b, sems.at[n]) for n, (a, b) in enumerate(zip(ins, rest))]
    back = [pltpu.make_async_copy(a, b, sems.at[7 + n]) for n, (a, b) in enumerate(zip(rest[7:13], outs))]
    for copy in copies:
        copy.start()
    dest, node, dist, wd, w_in, cells_in, w_src = rest[:7]
    cells, width = grid_h.shape
    rows = own.shape[0]
    for copy in copies[:4]:
        copy.wait()
    slot = jnp.zeros((1, cells), jnp.int32)
    for s, patch in enumerate(around_patch(n_lon)):
        slot = jnp.where(dest[1:2, :] == patch, s, slot)
    key[...] = slot * rows + node[1:2, :]
    back[2].start()
    half_wd = 0.5 * wd[...]
    lengths = dist[...].T
    for copy in copies[4:]:
        copy.wait()
    for c in range(0, cells, step):
        cut = slice(c, c + step)
        half = 0.5 * lax.dot_general(
            cells_in[:, cut], w_in[...], (((0,), (0,)), ((), ())), preferred_element_type=F32
        )
        h = gate(half).astype(BF16)
        grid_h[cut, :] = h
        proj = 0.5 * mm(h, w_src[...])
        msg1[cut, :] = gate(proj + lengths[cut, 1:2] * half_wd).astype(BF16)
    back[0].start()
    back[1].start()
    for s, out in enumerate((own, pair, band)):
        ids = (first + s) * rows + lax.broadcasted_iota(jnp.int32, (rows, cells), 0)
        out[...] = mm((key[...] == ids).astype(BF16), msg1[...]).astype(BF16)
        back[3 + s].start()
    for copy in back:
        copy.wait()


def front_call(dest, node, dist, wd, w_in, cells_in, w_src, rows, n_lon, first, step=256):
    cells, width = cells_in.shape[1], w_in.shape[1]
    tall = jax.ShapeDtypeStruct((cells, width), BF16)
    patch = jax.ShapeDtypeStruct((rows, width), BF16)
    args = (dest, node, dist, wd, w_in, cells_in, w_src)
    shapes = (tall, tall, jax.ShapeDtypeStruct((1, cells), jnp.int32), patch, patch, patch)
    return pl.pallas_call(
        functools.partial(front_kernel, n_lon=n_lon, first=first, step=step),
        out_shape=shapes,
        in_specs=[HB] * 7,
        out_specs=(HB,) * 6,
        scratch_shapes=[pltpu.VMEM(a.shape, a.dtype) for a in args + shapes] + [pltpu.SemaphoreType.DMA((13,))],
        compiler_params=params(60),
        cost_estimate=cost(8 * rows * cells * width, 12 * cells * width, 2 * cells * width),
    )(*args)


def own_kernel(grid_h, node, dist, w_src, wd, own, msg, *, step):
    cells, width = grid_h.shape
    lengths = dist[...].T
    half_wd = 0.5 * wd[...]
    for c in range(0, cells, step):
        cut = slice(c, c + step)
        proj = 0.5 * mm(grid_h[cut, :], w_src[...])
        msg[cut, :] = gate(proj + lengths[cut, 0:1] * half_wd).astype(BF16)
    ids = lax.broadcasted_iota(jnp.int32, (own.shape[0], cells), 0)
    own[...] = mm((node[0:1, :] == ids).astype(BF16), msg[...])


def own_call(grid_h, node, dist, w_src, wd, rows, step=256):
    cells, width = grid_h.shape
    return pl.pallas_call(
        functools.partial(own_kernel, step=step),
        out_shape=jax.ShapeDtypeStruct((rows, width), F32),
        in_specs=[VM] * 5,
        out_specs=VM,
        scratch_shapes=[pltpu.VMEM((cells, width), BF16)],
        compiler_params=params(12),
        cost_estimate=cost(4 * rows * cells * width, 6 * cells * width, cells * width),
    )(grid_h, node, dist, w_src, wd)


def mesh_kernel(emb, own, s0, s1, s2, w_self, w_agg, w_send, mesh_h, send, spread):
    rows, width = emb.shape
    agg = own[...]
    for part in (s0, s1, s2):
        agg += part[...].astype(F32)
    agg = agg.astype(BF16)
    upd = mm(emb[...], w_self[...]) + mm(agg, w_agg[...])
    h = (emb[...].astype(F32) + gate(0.5 * upd)).astype(BF16)
    mesh_h[...] = h
    grouped(0.5 * mm(h, w_send[...]), spread, rows, width // LANE, width // LANE)
    send[...] = spread[...].astype(BF16)


def mesh_call(emb, own, sums, w_self, w_agg, w_send):
    rows, width = emb.shape
    flat = (rows * width // LANE, LANE)
    return pl.pallas_call(
        mesh_kernel,
        out_shape=(jax.ShapeDtypeStruct((rows, width), BF16), jax.ShapeDtypeStruct(flat, BF16)),
        in_specs=[VM] * 8,
        out_specs=(VM, VM),
        scratch_shapes=[pltpu.VMEM(flat, F32)],
        compiler_params=params(8),
        cost_estimate=cost(6 * rows * width * width, 16 * rows * width, rows * width),
    )(emb, own, *sums, w_self, w_agg, w_send)


def recv_kernel(mesh_h, dist, w_recv, w_self, wd, recv, upd):
    rows, width = mesh_h.shape
    lanes = width // LANE
    degree = dist.shape[0]
    half = 0.5 * mm(mesh_h[...], w_recv[...])
    lengths = dist[...].T
    for j in range(degree):
        grouped(half + lengths[:, j : j + 1] * wd[...], recv, rows, lanes, degree * lanes, j * lanes)
    upd[...] = mm(mesh_h[...], w_self[...])


def recv_call(mesh_h, dist, w_recv, w_self, wd):
    rows, width = mesh_h.shape
    degree = dist.shape[0]
    return pl.pallas_call(
        recv_kernel,
        out_shape=(
            jax.ShapeDtypeStruct((rows * degree * width // LANE, LANE), F32),
            jax.ShapeDtypeStruct((rows, width), F32),
        ),
        in_specs=[VM] * 5,
        out_specs=(VM, VM),
        compiler_params=params(8),
        cost_estimate=cost(4 * rows * width * width, 40 * rows * width),
    )(mesh_h, dist, w_recv, w_self, wd)


def message_pair(tab, idx, a, b, recv, lanes, top):
    first = tab[pl.ds(idx[a] + 2 * lanes, 2 * lanes), :]
    second = tab[pl.ds(idx[b] + lanes, 2 * lanes), :]
    return gate(jnp.where(top, first, second) + recv)


def proc_kernel(idx, recv, *refs, unroll):
    blocks, (mesh_h, upd, w_agg, w_send, out, tab, acc) = refs[:9], refs[9:]
    rows, width = mesh_h.shape
    lanes = width // LANE
    two = 2 * lanes
    degree = idx.shape[0] // rows
    for s, b in enumerate(blocks):
        widen(tab, lanes * (2 + s * rows), b)
    top = lax.broadcasted_iota(jnp.int32, (two, LANE), 0) < lanes

    def node(n):
        total = None
        for j in range(0, degree, 2):
            add = recv[pl.ds(pl.multiple_of((n * degree + j) * lanes, two), two), :]
            msg = message_pair(tab, idx, j * rows + n, (j + 1) * rows + n, add, lanes, top)
            total = msg if total is None else total + msg
        acc[pl.ds(pl.multiple_of(n * two, two), two), :] = total

    def some(i, carry):
        for u in range(unroll):
            node(i * unroll + u)
        return carry

    lax.fori_loop(0, rows // unroll, some, 0)
    agg = [
        (acc[pl.ds(k, rows, stride=two), :] + acc[pl.ds(k + lanes, rows, stride=two), :]).astype(BF16)
        for k in range(lanes)
    ]
    total = upd[...] + mm(jnp.concatenate(agg, axis=1), w_agg[...])
    mesh_out = (mesh_h[...].astype(F32) + gate(0.5 * total)).astype(BF16)
    spread = acc.at[pl.ds(0, rows * lanes), :]
    grouped(0.5 * mm(mesh_out, w_send[...]), spread, rows, lanes, lanes)
    out[...] = spread[...].astype(BF16)


def proc_call(idx, recv, blocks, mesh_h, upd, w_agg, w_send):
    rows, width = mesh_h.shape
    lanes = width // LANE
    return pl.pallas_call(
        functools.partial(proc_kernel, unroll=16),
        out_shape=jax.ShapeDtypeStruct((rows * lanes, LANE), BF16),
        in_specs=[SM] + [VM] * 14,
        out_specs=VM,
        scratch_shapes=[
            pltpu.VMEM((lanes * (9 * rows + 4), LANE), F32),
            pltpu.VMEM((rows * 2 * lanes, LANE), F32),
        ],
        compiler_params=params(16),
        cost_estimate=cost(4 * rows * width * width, 32 * rows * width, idx.size * width),
    )(idx, recv, *blocks, mesh_h, upd, w_agg, w_send)


def cell_kernel(grid_h, dist, w_recv, w_self, wd, recv0, recv1, upd, *, step):
    cells, width = grid_h.shape
    lanes = width // LANE
    lengths = dist[...].T
    for c in range(0, cells, step):
        cut = slice(c, c + step)
        half = 0.5 * mm(grid_h[cut, :], w_recv[...])
        for k, recv in enumerate((recv0, recv1)):
            grouped(half + lengths[cut, k : k + 1] * wd[...], recv, step, lanes, lanes, c * lanes)
        upd[cut, :] = mm(grid_h[cut, :], w_self[...])


def cell_call(grid_h, dist, w_recv, w_self, wd, step=256):
    cells, width = grid_h.shape
    lanes = width // LANE
    flat = jax.ShapeDtypeStruct((cells * lanes, LANE), F32)
    return pl.pallas_call(
        functools.partial(cell_kernel, step=step),
        out_shape=(flat, flat, jax.ShapeDtypeStruct((cells, width), F32)),
        in_specs=[VM] * 5,
        out_specs=(VM,) * 3,
        compiler_params=params(8),
        cost_estimate=cost(4 * cells * width * width, 14 * cells * width),
    )(grid_h, dist, w_recv, w_self, wd)


def cells_kernel(idx, recv, upd, w_agg, *refs, n_blocks, step, unroll):
    blocks, refs = refs[:n_blocks], refs[n_blocks:]
    tab, acc = refs[-2:]
    cells, width = upd.shape
    lanes = width // LANE
    two = 2 * lanes
    size = blocks[0].shape[0]
    for s, b in enumerate(blocks):
        widen(tab, two + s * size, b)
    top = lax.broadcasted_iota(jnp.int32, (two, LANE), 0) < lanes

    def chunk(i, carry):
        base = pl.multiple_of(i * step, step)

        def some(q, carry):
            for u in range(unroll):
                c = (q * unroll + u) * 2
                add = recv[pl.ds(pl.multiple_of((base + c) * lanes, two), two), :]
                msg = message_pair(tab, idx, base + c, base + c + 1, add, lanes, top)
                acc[pl.ds(pl.multiple_of(c * lanes, two), two), :] = msg
            return carry

        lax.fori_loop(0, step // (2 * unroll), some, 0)
        agg = [acc[pl.ds(k, step, stride=lanes), :].astype(BF16) for k in range(lanes)]
        total = upd[pl.ds(base, step), :] + mm(jnp.concatenate(agg, axis=1), w_agg[...])
        if len(refs) == 3:
            refs[0][pl.ds(base, step), :] = total
            return carry
        cells_in, w_out, out = refs[:3]
        z = gate(0.5 * total).astype(BF16)
        change = lax.dot_general(w_out[...], z, (((1,), (1,)), ((), ())), preferred_element_type=F32)
        cut = pl.ds(base, step)
        out[:, cut] = (cells_in[:, cut].astype(F32) + change).astype(BF16)
        return carry

    lax.fori_loop(0, cells // step, chunk, 0)


def cells_call(idx, recv, upd, w_agg, blocks, last=(), step=512):
    cells, width = upd.shape
    lanes = width // LANE
    shape = jax.ShapeDtypeStruct(last[0].shape, BF16) if last else jax.ShapeDtypeStruct(upd.shape, F32)
    return pl.pallas_call(
        functools.partial(cells_kernel, n_blocks=len(blocks), step=step, unroll=32),
        out_shape=shape,
        in_specs=[SM] + [VM] * (3 + len(blocks) + len(last)),
        out_specs=VM,
        scratch_shapes=[
            pltpu.VMEM((sum(b.shape[0] for b in blocks) + 4 * lanes, LANE), F32),
            pltpu.VMEM((step * lanes, LANE), F32),
        ],
        compiler_params=params(8 + len(blocks) * 2),
        cost_estimate=cost(4 * cells * width * width, 16 * cells * width, 2 * cells * width),
    )(idx, recv, upd, w_agg, *blocks, *last)


def with_done(*blocks):
    return lax.optimization_barrier(blocks)


def shards(
    grid_in,
    mesh_emb,
    enc_dest,
    enc_node,
    enc_dist,
    dec_dist,
    mesh_src,
    proc_dist,
    w_grid_in,
    w_enc_src,
    w_enc_dist,
    w_mesh_self,
    w_mesh_agg,
    w_proc_send,
    w_proc_recv,
    w_proc_dist,
    w_proc_self,
    w_proc_agg,
    w_dec_send,
    w_dec_recv,
    w_dec_dist,
    w_grid_self,
    w_grid_agg,
    w_grid_out,
):
    width = w_grid_in.shape[1]
    lanes = width // LANE
    rows = mesh_emb.shape[0]
    where = (lax.axis_size("lon"), lax.axis_index("lat"), lax.axis_index("lon"))
    cells_in, dest, node = grid_in.T, enc_dest.T, enc_node.T

    enc_wd, lengths = w_enc_dist[None], enc_dist.T
    grid_h, msg1, far_key, z_own, z_pair, z_band = front_call(
        dest, node, lengths, enc_wd, w_grid_in, cells_in, w_enc_src, rows, where[0], 6
    )

    def partial(slot, messages):
        ids = slot * rows + lax.broadcasted_iota(jnp.int32, (rows, 1), 0)
        return mm((far_key == ids).astype(BF16), messages).astype(BF16)

    z_pair, z_band = across_pair(z_pair), across_band(z_band)
    p_own = partial(3, msg1)
    z_pair, messages = with_done(z_pair, msg1)
    z_sum = (z_own.astype(F32) + z_pair.astype(F32) + z_band.astype(F32)).astype(BF16)
    z_in = two_columns(z_sum, -1)
    p_band, p_pair = across_band(partial(5, messages)), across_pair(partial(4, messages))
    p_sum = (p_own.astype(F32) + p_pair.astype(F32) + p_band.astype(F32) + z_in.astype(F32)).astype(BF16)
    o_pair, o_band = across_pair(partial(1, messages)), across_band(partial(2, messages))
    p_sum, grid_h = with_done(p_sum, grid_h)
    own = own_call(grid_h, node, lengths, w_enc_src, enc_wd, rows)
    recv0, recv1, grid_upd = cell_call(grid_h, dec_dist.T, w_dec_recv, w_grid_self, (0.5 * w_dec_dist)[None])
    source = mesh_src.T
    proc_idx = ((slot_of(source // rows, *where) * rows + source % rows) * lanes).reshape(-1)
    near_idx, far_idx = node[0] * lanes, far_key[0] * lanes - rows * lanes
    p_in, own, recv0, recv1, grid_upd, proc_idx, near_idx, far_idx = with_done(
        across_columns(p_sum), own, recv0, recv1, grid_upd, proc_idx, near_idx, far_idx
    )
    mesh_h, proc_send = mesh_call(mesh_emb, own, (o_pair, o_band, p_in), w_mesh_self, w_mesh_agg, w_proc_send)

    pair_col = across_columns(proc_send)
    recv, mesh_upd = recv_call(mesh_h, proc_dist.T, w_proc_recv, w_proc_self, (0.5 * w_proc_dist)[None])
    pair_col, recv, mesh_upd = with_done(pair_col, recv, mesh_upd)
    nearby = halo(proc_send, pair_col)
    dec_send = proc_call(proc_idx, recv, nearby, mesh_h, mesh_upd, w_proc_agg, w_dec_send)

    pair_col = across_columns(dec_send)
    grid_upd = cells_call(near_idx, recv0, grid_upd, w_grid_agg, [dec_send])
    pair_col, grid_upd = with_done(pair_col, grid_upd)
    around = halo(dec_send, pair_col)[1:]
    pred = cells_call(far_idx, recv1, grid_upd, w_grid_agg, around, (cells_in, w_grid_out.T))
    return pred.T


def solution(mesh):
    split = P(("lat", "lon"), None)
    in_specs = (split,) * 8 + (P(),) * 16
    return jax.shard_map(shards, mesh=mesh, in_specs=in_specs, out_specs=split, check_vma=False)
```

```python
import functools

import jax
import jax.numpy as jnp
from jax import lax
from jax.experimental import pallas as pl
from jax.experimental.pallas import tpu as pltpu
from jax.sharding import PartitionSpec as P

F32, BF16 = jnp.float32, jnp.bfloat16
LANE = 128
VM = pl.BlockSpec(memory_space=pltpu.VMEM)
SM = pl.BlockSpec(memory_space=pltpu.SMEM)
HB = pl.BlockSpec(memory_space=pltpu.HBM)


def mm(a, b):
    return jnp.dot(a, b, preferred_element_type=F32)


def gate(half):
    return half * jnp.tanh(half) + half


def across_pair(block):
    n = lax.axis_size("lat")
    return lax.ppermute(block, "lat", [(i, i ^ 1) for i in range(n)])


def across_band(block):
    n = lax.axis_size("lat")
    pairs = []
    for i in range(1, n - 1, 2):
        pairs += [(i, i + 1), (i + 1, i)]
    return lax.ppermute(block, "lat", pairs)


def across_columns(block):
    n = lax.axis_size("lon")
    return lax.ppermute(block, "lon", [(i, i ^ 1) for i in range(n)])


def two_columns(block, sign):
    n = lax.axis_size("lon")
    pairs = [(i, (i + (2 * sign if i % 2 == 0 else -2 * sign)) % n) for i in range(n)]
    return lax.ppermute(block, "lon", pairs)


def slot_of(patch, n_lon, my_lat, my_lon):
    row, col = patch // n_lon, patch % n_lon
    row_slot = jnp.where(row == my_lat, 0, jnp.where(row == (my_lat ^ 1), 1, 2))
    col_slot = jnp.where(col == my_lon, 0, jnp.where(col == (my_lon ^ 1), 1, 2))
    return col_slot * 3 + row_slot


def with_done(*blocks):
    return lax.optimization_barrier(blocks)


def halo(own, *work):
    *work, own_band, pair_col = with_done(*work, across_band(own), across_columns(own))
    far_col = two_columns(pair_col, 1)
    pc_band = across_band(pair_col)
    own_pair = across_pair(own)
    pc_pair = across_pair(pair_col)
    fc_band = across_band(far_col)
    fc_pair = across_pair(far_col)
    return [own, own_pair, own_band, pair_col, pc_pair, pc_band, far_col, fc_pair, fc_band], work


def params(mib):
    return pltpu.CompilerParams(vmem_limit_bytes=mib * 2**20)


def cost(flops, moved, exps=0):
    return pl.CostEstimate(flops=flops, bytes_accessed=moved, transcendentals=exps)


def grouped(full, spread, rows, lanes, every, first=0):
    for k in range(lanes):
        spread[pl.ds(first + k, rows, stride=every), :] = full[:, k * LANE : (k + 1) * LANE]


def widen(tab, base, block, step=256):
    def go(i, carry):
        r = pl.multiple_of(i * step, step)
        tab[pl.ds(base + r, step), :] = block[pl.ds(r, step), :].astype(F32)
        return carry

    lax.fori_loop(0, block.shape[0] // step, go, 0)


def around_patch(n_lon):
    row, col = lax.axis_index("lat"), lax.axis_index("lon")
    side = lax.rem(row, 2) * 2 - 1
    turn = lax.rem(col, 2) * 2 - 1
    return [
        r * n_lon + lax.rem(c + n_lon, n_lon)
        for c in (col, col - turn, col + turn)
        for r in (row, row - side, row + side)
    ]


def front_kernel(*refs, n_lon, first, step):
    ins, outs, rest = refs[:7], refs[7:13], refs[13:]
    grid_h, msg1, key, own, pair, band = rest[7:13]
    sems = rest[13]
    copies = [pltpu.make_async_copy(a, b, sems.at[n]) for n, (a, b) in enumerate(zip(ins, rest))]
    back = [pltpu.make_async_copy(a, b, sems.at[7 + n]) for n, (a, b) in enumerate(zip(rest[7:13], outs))]
    for copy in copies:
        copy.start()
    dest, node, dist, wd, w_in, cells_in, w_src = rest[:7]
    cells, width = grid_h.shape
    rows = own.shape[0]
    for copy in copies[:4]:
        copy.wait()
    slot = jnp.zeros((1, cells), jnp.int32)
    for s, patch in enumerate(around_patch(n_lon)):
        slot = jnp.where(dest[1:2, :] == patch, s, slot)
    key[...] = slot * rows + node[1:2, :]
    back[2].start()
    half_wd = 0.5 * wd[...]
    lengths = dist[...].T
    for copy in copies[4:]:
        copy.wait()
    for c in range(0, cells, step):
        cut = slice(c, c + step)
        half = 0.5 * lax.dot_general(
            cells_in[:, cut], w_in[...], (((0,), (0,)), ((), ())), preferred_element_type=F32
        )
        h = gate(half).astype(BF16)
        grid_h[cut, :] = h
        proj = 0.5 * mm(h, w_src[...])
        msg1[cut, :] = gate(proj + lengths[cut, 1:2] * half_wd).astype(BF16)
    back[0].start()
    back[1].start()
    for s, out in enumerate((own, pair, band)):
        ids = (first + s) * rows + lax.broadcasted_iota(jnp.int32, (rows, cells), 0)
        out[...] = mm((key[...] == ids).astype(BF16), msg1[...]).astype(BF16)
        back[3 + s].start()
    for copy in back:
        copy.wait()


def front_call(dest, node, dist, wd, w_in, cells_in, w_src, rows, n_lon, first, step=256):
    cells, width = cells_in.shape[1], w_in.shape[1]
    tall = jax.ShapeDtypeStruct((cells, width), BF16)
    patch = jax.ShapeDtypeStruct((rows, width), BF16)
    args = (dest, node, dist, wd, w_in, cells_in, w_src)
    shapes = (tall, tall, jax.ShapeDtypeStruct((1, cells), jnp.int32), patch, patch, patch)
    return pl.pallas_call(
        functools.partial(front_kernel, n_lon=n_lon, first=first, step=step),
        out_shape=shapes,
        in_specs=[HB] * 7,
        out_specs=(HB,) * 6,
        scratch_shapes=[pltpu.VMEM(a.shape, a.dtype) for a in args + shapes] + [pltpu.SemaphoreType.DMA((13,))],
        compiler_params=params(60),
        cost_estimate=cost(8 * rows * cells * width, 12 * cells * width, 2 * cells * width),
    )(*args)


def own_kernel(grid_h, node, dist, w_src, wd, own, msg, *, step):
    cells, width = grid_h.shape
    lengths = dist[...].T
    half_wd = 0.5 * wd[...]
    for c in range(0, cells, step):
        cut = slice(c, c + step)
        proj = 0.5 * mm(grid_h[cut, :], w_src[...])
        msg[cut, :] = gate(proj + lengths[cut, 0:1] * half_wd).astype(BF16)
    ids = lax.broadcasted_iota(jnp.int32, (own.shape[0], cells), 0)
    own[...] = mm((node[0:1, :] == ids).astype(BF16), msg[...])


def own_call(grid_h, node, dist, w_src, wd, rows, step=256):
    cells, width = grid_h.shape
    return pl.pallas_call(
        functools.partial(own_kernel, step=step),
        out_shape=jax.ShapeDtypeStruct((rows, width), F32),
        in_specs=[VM] * 5,
        out_specs=VM,
        scratch_shapes=[pltpu.VMEM((cells, width), BF16)],
        compiler_params=params(12),
        cost_estimate=cost(4 * rows * cells * width, 6 * cells * width, cells * width),
    )(grid_h, node, dist, w_src, wd)


def mesh_kernel(emb, own, s0, s1, s2, w_self, w_agg, w_send, mesh_h, send, spread):
    rows, width = emb.shape
    agg = own[...]
    for part in (s0, s1, s2):
        agg += part[...].astype(F32)
    agg = agg.astype(BF16)
    upd = mm(emb[...], w_self[...]) + mm(agg, w_agg[...])
    h = (emb[...].astype(F32) + gate(0.5 * upd)).astype(BF16)
    mesh_h[...] = h
    grouped(0.5 * mm(h, w_send[...]), spread, rows, width // LANE, width // LANE)
    send[...] = spread[...].astype(BF16)


def mesh_call(emb, own, sums, w_self, w_agg, w_send):
    rows, width = emb.shape
    flat = (rows * width // LANE, LANE)
    return pl.pallas_call(
        mesh_kernel,
        out_shape=(jax.ShapeDtypeStruct((rows, width), BF16), jax.ShapeDtypeStruct(flat, BF16)),
        in_specs=[VM] * 8,
        out_specs=(VM, VM),
        scratch_shapes=[pltpu.VMEM(flat, F32)],
        compiler_params=params(8),
        cost_estimate=cost(6 * rows * width * width, 16 * rows * width, rows * width),
    )(emb, own, *sums, w_self, w_agg, w_send)


def recv_kernel(mesh_h, dist, w_recv, w_self, wd, recv, upd):
    rows, width = mesh_h.shape
    lanes = width // LANE
    degree = dist.shape[0]
    half = 0.5 * mm(mesh_h[...], w_recv[...])
    lengths = dist[...].T
    for j in range(degree):
        grouped(half + lengths[:, j : j + 1] * wd[...], recv, rows, lanes, degree * lanes, j * lanes)
    upd[...] = mm(mesh_h[...], w_self[...])


def recv_call(mesh_h, dist, w_recv, w_self, wd):
    rows, width = mesh_h.shape
    degree = dist.shape[0]
    return pl.pallas_call(
        recv_kernel,
        out_shape=(
            jax.ShapeDtypeStruct((rows * degree * width // LANE, LANE), F32),
            jax.ShapeDtypeStruct((rows, width), F32),
        ),
        in_specs=[VM] * 5,
        out_specs=(VM, VM),
        compiler_params=params(8),
        cost_estimate=cost(4 * rows * width * width, 40 * rows * width),
    )(mesh_h, dist, w_recv, w_self, wd)


def message_pair(tab, idx, a, b, recv, lanes, top):
    first = tab[pl.ds(idx[a] + 2 * lanes, 2 * lanes), :]
    second = tab[pl.ds(idx[b] + lanes, 2 * lanes), :]
    return gate(jnp.where(top, first, second) + recv)


def proc_kernel(idx, recv, *refs, unroll):
    blocks, (mesh_h, upd, w_agg, w_send, out, tab, acc) = refs[:9], refs[9:]
    rows, width = mesh_h.shape
    lanes = width // LANE
    two = 2 * lanes
    degree = idx.shape[0] // rows
    for s, b in enumerate(blocks):
        widen(tab, lanes * (2 + s * rows), b)
    top = lax.broadcasted_iota(jnp.int32, (two, LANE), 0) < lanes

    def node(n):
        total = None
        for j in range(0, degree, 2):
            add = recv[pl.ds(pl.multiple_of((n * degree + j) * lanes, two), two), :]
            msg = message_pair(tab, idx, j * rows + n, (j + 1) * rows + n, add, lanes, top)
            total = msg if total is None else total + msg
        acc[pl.ds(pl.multiple_of(n * two, two), two), :] = total

    def some(i, carry):
        for u in range(unroll):
            node(i * unroll + u)
        return carry

    lax.fori_loop(0, rows // unroll, some, 0)
    agg = [
        (acc[pl.ds(k, rows, stride=two), :] + acc[pl.ds(k + lanes, rows, stride=two), :]).astype(BF16)
        for k in range(lanes)
    ]
    total = upd[...] + mm(jnp.concatenate(agg, axis=1), w_agg[...])
    mesh_out = (mesh_h[...].astype(F32) + gate(0.5 * total)).astype(BF16)
    spread = acc.at[pl.ds(0, rows * lanes), :]
    grouped(0.5 * mm(mesh_out, w_send[...]), spread, rows, lanes, lanes)
    out[...] = spread[...].astype(BF16)


def proc_call(idx, recv, blocks, mesh_h, upd, w_agg, w_send):
    rows, width = mesh_h.shape
    lanes = width // LANE
    return pl.pallas_call(
        functools.partial(proc_kernel, unroll=16),
        out_shape=jax.ShapeDtypeStruct((rows * lanes, LANE), BF16),
        in_specs=[SM] + [VM] * 14,
        out_specs=VM,
        scratch_shapes=[
            pltpu.VMEM((lanes * (9 * rows + 4), LANE), F32),
            pltpu.VMEM((rows * 2 * lanes, LANE), F32),
        ],
        compiler_params=params(16),
        cost_estimate=cost(4 * rows * width * width, 32 * rows * width, idx.size * width),
    )(idx, recv, *blocks, mesh_h, upd, w_agg, w_send)


def cell_kernel(grid_h, dist, w_recv, w_self, wd, recv0, recv1, upd, *, step):
    cells, width = grid_h.shape
    lanes = width // LANE
    lengths = dist[...].T
    for c in range(0, cells, step):
        cut = slice(c, c + step)
        half = 0.5 * mm(grid_h[cut, :], w_recv[...])
        for k, recv in enumerate((recv0, recv1)):
            grouped(half + lengths[cut, k : k + 1] * wd[...], recv, step, lanes, lanes, c * lanes)
        upd[cut, :] = mm(grid_h[cut, :], w_self[...])


def cell_call(grid_h, dist, w_recv, w_self, wd, step=256):
    cells, width = grid_h.shape
    lanes = width // LANE
    flat = jax.ShapeDtypeStruct((cells * lanes, LANE), F32)
    return pl.pallas_call(
        functools.partial(cell_kernel, step=step),
        out_shape=(flat, flat, jax.ShapeDtypeStruct((cells, width), F32)),
        in_specs=[VM] * 5,
        out_specs=(VM,) * 3,
        compiler_params=params(8),
        cost_estimate=cost(4 * cells * width * width, 14 * cells * width),
    )(grid_h, dist, w_recv, w_self, wd)


def cells_kernel(idx, recv, upd, w_agg, *refs, n_blocks, step, unroll):
    blocks, refs = refs[:n_blocks], refs[n_blocks:]
    tab, acc = refs[-2:]
    cells, width = upd.shape
    lanes = width // LANE
    two = 2 * lanes
    size = blocks[0].shape[0]
    for s, b in enumerate(blocks):
        widen(tab, two + s * size, b)
    top = lax.broadcasted_iota(jnp.int32, (two, LANE), 0) < lanes

    def chunk(i, carry):
        base = pl.multiple_of(i * step, step)

        def some(q, carry):
            for u in range(unroll):
                c = (q * unroll + u) * 2
                add = recv[pl.ds(pl.multiple_of((base + c) * lanes, two), two), :]
                msg = message_pair(tab, idx, base + c, base + c + 1, add, lanes, top)
                acc[pl.ds(pl.multiple_of(c * lanes, two), two), :] = msg
            return carry

        lax.fori_loop(0, step // (2 * unroll), some, 0)
        agg = [acc[pl.ds(k, step, stride=lanes), :].astype(BF16) for k in range(lanes)]
        total = upd[pl.ds(base, step), :] + mm(jnp.concatenate(agg, axis=1), w_agg[...])
        if len(refs) == 3:
            refs[0][pl.ds(base, step), :] = total
            return carry
        cells_in, w_out, out = refs[:3]
        z = gate(0.5 * total).astype(BF16)
        change = lax.dot_general(w_out[...], z, (((1,), (1,)), ((), ())), preferred_element_type=F32)
        cut = pl.ds(base, step)
        out[:, cut] = (cells_in[:, cut].astype(F32) + change).astype(BF16)
        return carry

    lax.fori_loop(0, cells // step, chunk, 0)


def cells_call(idx, recv, upd, w_agg, blocks, last=(), step=1024):
    cells, width = upd.shape
    lanes = width // LANE
    shape = jax.ShapeDtypeStruct(last[0].shape, BF16) if last else jax.ShapeDtypeStruct(upd.shape, F32)
    return pl.pallas_call(
        functools.partial(cells_kernel, n_blocks=len(blocks), step=step, unroll=32),
        out_shape=shape,
        in_specs=[SM] + [VM] * (3 + len(blocks) + len(last)),
        out_specs=VM,
        scratch_shapes=[
            pltpu.VMEM((sum(b.shape[0] for b in blocks) + 4 * lanes, LANE), F32),
            pltpu.VMEM((step * lanes, LANE), F32),
        ],
        compiler_params=params(8 + len(blocks) * 2),
        cost_estimate=cost(4 * cells * width * width, 16 * cells * width, 2 * cells * width),
    )(idx, recv, upd, w_agg, *blocks, *last)


def shards(
    grid_in,
    mesh_emb,
    enc_dest,
    enc_node,
    enc_dist,
    dec_dist,
    mesh_src,
    proc_dist,
    w_grid_in,
    w_enc_src,
    w_enc_dist,
    w_mesh_self,
    w_mesh_agg,
    w_proc_send,
    w_proc_recv,
    w_proc_dist,
    w_proc_self,
    w_proc_agg,
    w_dec_send,
    w_dec_recv,
    w_dec_dist,
    w_grid_self,
    w_grid_agg,
    w_grid_out,
):
    width = w_grid_in.shape[1]
    lanes = width // LANE
    rows = mesh_emb.shape[0]
    where = (lax.axis_size("lon"), lax.axis_index("lat"), lax.axis_index("lon"))
    cells_in, dest, node = grid_in.T, enc_dest.T, enc_node.T

    enc_wd, lengths = w_enc_dist[None], enc_dist.T
    grid_h, msg1, far_key, z_own, z_pair, z_band = front_call(
        dest, node, lengths, enc_wd, w_grid_in, cells_in, w_enc_src, rows, where[0], 6
    )

    def partial(slot, messages):
        ids = slot * rows + lax.broadcasted_iota(jnp.int32, (rows, 1), 0)
        return mm((far_key == ids).astype(BF16), messages).astype(BF16)

    z_pair, z_band = across_pair(z_pair), across_band(z_band)
    p_own = partial(3, msg1)
    z_pair, messages = with_done(z_pair, msg1)
    z_sum = (z_own.astype(F32) + z_pair.astype(F32) + z_band.astype(F32)).astype(BF16)
    z_in = two_columns(z_sum, -1)
    p_band, p_pair = across_band(partial(5, messages)), across_pair(partial(4, messages))
    p_sum = (p_own.astype(F32) + p_pair.astype(F32) + p_band.astype(F32) + z_in.astype(F32)).astype(BF16)
    o_pair, o_band = across_pair(partial(1, messages)), across_band(partial(2, messages))
    p_sum, grid_h = with_done(p_sum, grid_h)
    own = own_call(grid_h, node, lengths, w_enc_src, enc_wd, rows)
    recv0, recv1, grid_upd = cell_call(grid_h, dec_dist.T, w_dec_recv, w_grid_self, (0.5 * w_dec_dist)[None])
    source = mesh_src.T
    proc_idx = ((slot_of(source // rows, *where) * rows + source % rows) * lanes).reshape(-1)
    near_idx, far_idx = node[0] * lanes, far_key[0] * lanes - rows * lanes
    p_in, own, recv0, recv1, grid_upd, proc_idx, near_idx, far_idx = with_done(
        across_columns(p_sum), own, recv0, recv1, grid_upd, proc_idx, near_idx, far_idx
    )
    mesh_h, proc_send = mesh_call(mesh_emb, own, (o_pair, o_band, p_in), w_mesh_self, w_mesh_agg, w_proc_send)

    recv, mesh_upd = recv_call(mesh_h, proc_dist.T, w_proc_recv, w_proc_self, (0.5 * w_proc_dist)[None])
    nearby, (recv, mesh_upd) = halo(proc_send, recv, mesh_upd)
    dec_send = proc_call(proc_idx, recv, nearby, mesh_h, mesh_upd, w_proc_agg, w_dec_send)

    grid_upd = cells_call(near_idx, recv0, grid_upd, w_grid_agg, [dec_send])
    around, (grid_upd,) = halo(dec_send, grid_upd)
    pred = cells_call(far_idx, recv1, grid_upd, w_grid_agg, around[1:], (cells_in, w_grid_out.T))
    return pred.T


def solution(mesh):
    split = P(("lat", "lon"), None)
    in_specs = (split,) * 8 + (P(),) * 16
    return jax.shard_map(shards, mesh=mesh, in_specs=in_specs, out_specs=split, check_vma=False)
```

```python
import functools

import jax
import jax.numpy as jnp
from jax import lax
from jax.experimental import pallas as pl
from jax.experimental.pallas import tpu as pltpu
from jax.sharding import PartitionSpec as P

F32, BF16 = jnp.float32, jnp.bfloat16
LANE = 128
VM = pl.BlockSpec(memory_space=pltpu.VMEM)
SM = pl.BlockSpec(memory_space=pltpu.SMEM)
HB = pl.BlockSpec(memory_space=pltpu.HBM)


def mm(a, b):
    return jnp.dot(a, b, preferred_element_type=F32)


def gate(half):
    return half * jnp.tanh(half) + half


def across_pair(block):
    n = lax.axis_size("lat")
    return lax.ppermute(block, "lat", [(i, i ^ 1) for i in range(n)])


def across_band(block):
    n = lax.axis_size("lat")
    pairs = []
    for i in range(1, n - 1, 2):
        pairs += [(i, i + 1), (i + 1, i)]
    return lax.ppermute(block, "lat", pairs)


def across_columns(block):
    n = lax.axis_size("lon")
    return lax.ppermute(block, "lon", [(i, i ^ 1) for i in range(n)])


def two_columns(block, sign):
    n = lax.axis_size("lon")
    pairs = [(i, (i + (2 * sign if i % 2 == 0 else -2 * sign)) % n) for i in range(n)]
    return lax.ppermute(block, "lon", pairs)


def slot_of(patch, n_lon, my_lat, my_lon):
    row, col = patch // n_lon, patch % n_lon
    row_slot = jnp.where(row == my_lat, 0, jnp.where(row == (my_lat ^ 1), 1, 2))
    col_slot = jnp.where(col == my_lon, 0, jnp.where(col == (my_lon ^ 1), 1, 2))
    return col_slot * 3 + row_slot


def with_done(*blocks):
    return lax.optimization_barrier(blocks)


def halo(own, *work):
    *work, own_band, pair_col = with_done(*work, across_band(own), across_columns(own))
    far_col = two_columns(pair_col, 1)
    pc_band = across_band(pair_col)
    own_pair = across_pair(own)
    pc_pair = across_pair(pair_col)
    fc_band = across_band(far_col)
    fc_pair = across_pair(far_col)
    return [own, own_pair, own_band, pair_col, pc_pair, pc_band, far_col, fc_pair, fc_band], work


def params(mib):
    return pltpu.CompilerParams(vmem_limit_bytes=mib * 2**20)


def cost(flops, moved, exps=0):
    return pl.CostEstimate(flops=flops, bytes_accessed=moved, transcendentals=exps)


def grouped(full, spread, rows, lanes, every, first=0):
    for k in range(lanes):
        spread[pl.ds(first + k, rows, stride=every), :] = full[:, k * LANE : (k + 1) * LANE]


def widen(tab, base, block, step=256):
    def go(i, carry):
        r = pl.multiple_of(i * step, step)
        tab[pl.ds(base + r, step), :] = block[pl.ds(r, step), :].astype(F32)
        return carry

    lax.fori_loop(0, block.shape[0] // step, go, 0)


def around_patch(n_lon):
    row, col = lax.axis_index("lat"), lax.axis_index("lon")
    side = lax.rem(row, 2) * 2 - 1
    turn = lax.rem(col, 2) * 2 - 1
    return [
        r * n_lon + lax.rem(c + n_lon, n_lon)
        for c in (col, col - turn, col + turn)
        for r in (row, row - side, row + side)
    ]


def front_kernel(*refs, n_lon, first, step):
    ins, outs, rest = refs[:7], refs[7:13], refs[13:]
    grid_h, msg1, key, own, pair, band = rest[7:13]
    sems = rest[13]
    copies = [pltpu.make_async_copy(a, b, sems.at[n]) for n, (a, b) in enumerate(zip(ins, rest))]
    back = [pltpu.make_async_copy(a, b, sems.at[7 + n]) for n, (a, b) in enumerate(zip(rest[7:13], outs))]
    for copy in copies:
        copy.start()
    dest, node, dist, wd, w_in, cells_in, w_src = rest[:7]
    cells, width = grid_h.shape
    rows = own.shape[0]
    for copy in copies[:4]:
        copy.wait()
    slot = jnp.zeros((1, cells), jnp.int32)
    for s, patch in enumerate(around_patch(n_lon)):
        slot = jnp.where(dest[1:2, :] == patch, s, slot)
    key[...] = slot * rows + node[1:2, :]
    back[2].start()
    half_wd = 0.5 * wd[...]
    lengths = dist[...].T
    for copy in copies[4:]:
        copy.wait()
    for c in range(0, cells, step):
        cut = slice(c, c + step)
        half = 0.5 * lax.dot_general(
            cells_in[:, cut], w_in[...], (((0,), (0,)), ((), ())), preferred_element_type=F32
        )
        h = gate(half).astype(BF16)
        grid_h[cut, :] = h
        proj = 0.5 * mm(h, w_src[...])
        msg1[cut, :] = gate(proj + lengths[cut, 1:2] * half_wd).astype(BF16)
    back[0].start()
    back[1].start()
    for s, out in enumerate((own, pair, band)):
        ids = (first + s) * rows + lax.broadcasted_iota(jnp.int32, (rows, cells), 0)
        out[...] = mm((key[...] == ids).astype(BF16), msg1[...]).astype(BF16)
        back[3 + s].start()
    for copy in back:
        copy.wait()


def front_call(dest, node, dist, wd, w_in, cells_in, w_src, rows, n_lon, first, step=256):
    cells, width = cells_in.shape[1], w_in.shape[1]
    tall = jax.ShapeDtypeStruct((cells, width), BF16)
    patch = jax.ShapeDtypeStruct((rows, width), BF16)
    args = (dest, node, dist, wd, w_in, cells_in, w_src)
    shapes = (tall, tall, jax.ShapeDtypeStruct((1, cells), jnp.int32), patch, patch, patch)
    return pl.pallas_call(
        functools.partial(front_kernel, n_lon=n_lon, first=first, step=step),
        out_shape=shapes,
        in_specs=[HB] * 7,
        out_specs=(HB,) * 6,
        scratch_shapes=[pltpu.VMEM(a.shape, a.dtype) for a in args + shapes] + [pltpu.SemaphoreType.DMA((13,))],
        compiler_params=params(60),
        cost_estimate=cost(8 * rows * cells * width, 12 * cells * width, 2 * cells * width),
    )(*args)


def own_kernel(grid_h, node, dist, w_src, wd, own, msg, *, step):
    cells, width = grid_h.shape
    lengths = dist[...].T
    half_wd = 0.5 * wd[...]
    for c in range(0, cells, step):
        cut = slice(c, c + step)
        proj = 0.5 * mm(grid_h[cut, :], w_src[...])
        msg[cut, :] = gate(proj + lengths[cut, 0:1] * half_wd).astype(BF16)
    ids = lax.broadcasted_iota(jnp.int32, (own.shape[0], cells), 0)
    own[...] = mm((node[0:1, :] == ids).astype(BF16), msg[...])


def own_call(grid_h, node, dist, w_src, wd, rows, step=256):
    cells, width = grid_h.shape
    return pl.pallas_call(
        functools.partial(own_kernel, step=step),
        out_shape=jax.ShapeDtypeStruct((rows, width), F32),
        in_specs=[VM] * 5,
        out_specs=VM,
        scratch_shapes=[pltpu.VMEM((cells, width), BF16)],
        compiler_params=params(12),
        cost_estimate=cost(4 * rows * cells * width, 6 * cells * width, cells * width),
    )(grid_h, node, dist, w_src, wd)


def mesh_kernel(emb, own, s0, s1, s2, w_self, w_agg, w_send, mesh_h, send, spread):
    rows, width = emb.shape
    agg = own[...]
    for part in (s0, s1, s2):
        agg += part[...].astype(F32)
    agg = agg.astype(BF16)
    upd = mm(emb[...], w_self[...]) + mm(agg, w_agg[...])
    h = (emb[...].astype(F32) + gate(0.5 * upd)).astype(BF16)
    mesh_h[...] = h
    grouped(0.5 * mm(h, w_send[...]), spread, rows, width // LANE, width // LANE)
    send[...] = spread[...].astype(BF16)


def mesh_call(emb, own, sums, w_self, w_agg, w_send):
    rows, width = emb.shape
    flat = (rows * width // LANE, LANE)
    return pl.pallas_call(
        mesh_kernel,
        out_shape=(jax.ShapeDtypeStruct((rows, width), BF16), jax.ShapeDtypeStruct(flat, BF16)),
        in_specs=[VM] * 8,
        out_specs=(VM, VM),
        scratch_shapes=[pltpu.VMEM(flat, F32)],
        compiler_params=params(8),
        cost_estimate=cost(6 * rows * width * width, 16 * rows * width, rows * width),
    )(emb, own, *sums, w_self, w_agg, w_send)


def recv_kernel(mesh_h, dist, w_recv, w_self, wd, recv, upd):
    rows, width = mesh_h.shape
    lanes = width // LANE
    degree = dist.shape[0]
    half = 0.5 * mm(mesh_h[...], w_recv[...])
    lengths = dist[...].T
    for j in range(degree):
        grouped(half + lengths[:, j : j + 1] * wd[...], recv, rows, lanes, degree * lanes, j * lanes)
    upd[...] = mm(mesh_h[...], w_self[...])


def recv_call(mesh_h, dist, w_recv, w_self, wd):
    rows, width = mesh_h.shape
    degree = dist.shape[0]
    return pl.pallas_call(
        recv_kernel,
        out_shape=(
            jax.ShapeDtypeStruct((rows * degree * width // LANE, LANE), F32),
            jax.ShapeDtypeStruct((rows, width), F32),
        ),
        in_specs=[VM] * 5,
        out_specs=(VM, VM),
        compiler_params=params(8),
        cost_estimate=cost(4 * rows * width * width, 40 * rows * width),
    )(mesh_h, dist, w_recv, w_self, wd)


def message_pair(tab, idx, a, b, recv, lanes, top):
    first = tab[pl.ds(idx[a] + 2 * lanes, 2 * lanes), :]
    second = tab[pl.ds(idx[b] + lanes, 2 * lanes), :]
    return gate(jnp.where(top, first, second) + recv)


def proc_kernel(idx, recv, *refs, unroll):
    blocks, (mesh_h, upd, w_agg, w_send, out, tab, acc) = refs[:9], refs[9:]
    rows, width = mesh_h.shape
    lanes = width // LANE
    two = 2 * lanes
    degree = idx.shape[0] // rows
    for s, b in enumerate(blocks):
        widen(tab, lanes * (2 + s * rows), b)
    top = lax.broadcasted_iota(jnp.int32, (two, LANE), 0) < lanes

    def node(n):
        total = None
        for j in range(0, degree, 2):
            add = recv[pl.ds(pl.multiple_of((n * degree + j) * lanes, two), two), :]
            msg = message_pair(tab, idx, j * rows + n, (j + 1) * rows + n, add, lanes, top)
            total = msg if total is None else total + msg
        acc[pl.ds(pl.multiple_of(n * two, two), two), :] = total

    def some(i, carry):
        for u in range(unroll):
            node(i * unroll + u)
        return carry

    lax.fori_loop(0, rows // unroll, some, 0)
    agg = [
        (acc[pl.ds(k, rows, stride=two), :] + acc[pl.ds(k + lanes, rows, stride=two), :]).astype(BF16)
        for k in range(lanes)
    ]
    total = upd[...] + mm(jnp.concatenate(agg, axis=1), w_agg[...])
    mesh_out = (mesh_h[...].astype(F32) + gate(0.5 * total)).astype(BF16)
    spread = acc.at[pl.ds(0, rows * lanes), :]
    grouped(0.5 * mm(mesh_out, w_send[...]), spread, rows, lanes, lanes)
    out[...] = spread[...].astype(BF16)


def proc_call(idx, recv, blocks, mesh_h, upd, w_agg, w_send):
    rows, width = mesh_h.shape
    lanes = width // LANE
    return pl.pallas_call(
        functools.partial(proc_kernel, unroll=16),
        out_shape=jax.ShapeDtypeStruct((rows * lanes, LANE), BF16),
        in_specs=[SM] + [VM] * 14,
        out_specs=VM,
        scratch_shapes=[
            pltpu.VMEM((lanes * (9 * rows + 4), LANE), F32),
            pltpu.VMEM((rows * 2 * lanes, LANE), F32),
        ],
        compiler_params=params(16),
        cost_estimate=cost(4 * rows * width * width, 32 * rows * width, idx.size * width),
    )(idx, recv, *blocks, mesh_h, upd, w_agg, w_send)


def cell_kernel(grid_h, dist, w_recv, w_self, wd, recv0, recv1, upd, *, step):
    cells, width = grid_h.shape
    lanes = width // LANE
    lengths = dist[...].T
    for c in range(0, cells, step):
        cut = slice(c, c + step)
        half = 0.5 * mm(grid_h[cut, :], w_recv[...])
        for k, recv in enumerate((recv0, recv1)):
            grouped(half + lengths[cut, k : k + 1] * wd[...], recv, step, lanes, lanes, c * lanes)
        upd[cut, :] = mm(grid_h[cut, :], w_self[...])


def cell_call(grid_h, dist, w_recv, w_self, wd, step=256):
    cells, width = grid_h.shape
    lanes = width // LANE
    flat = jax.ShapeDtypeStruct((cells * lanes, LANE), F32)
    return pl.pallas_call(
        functools.partial(cell_kernel, step=step),
        out_shape=(flat, flat, jax.ShapeDtypeStruct((cells, width), F32)),
        in_specs=[VM] * 5,
        out_specs=(VM,) * 3,
        compiler_params=params(8),
        cost_estimate=cost(4 * cells * width * width, 14 * cells * width),
    )(grid_h, dist, w_recv, w_self, wd)


def cells_kernel(idx, recv, upd, w_agg, *refs, n_blocks, step, unroll):
    blocks, refs = refs[:n_blocks], refs[n_blocks:]
    tab, acc = refs[-2:]
    cells, width = upd.shape
    lanes = width // LANE
    two = 2 * lanes
    size = blocks[0].shape[0]
    for s, b in enumerate(blocks):
        widen(tab, two + s * size, b)
    top = lax.broadcasted_iota(jnp.int32, (two, LANE), 0) < lanes

    def chunk(i, carry):
        base = pl.multiple_of(i * step, step)

        def some(q, carry):
            for u in range(unroll):
                c = (q * unroll + u) * 2
                add = recv[pl.ds(pl.multiple_of((base + c) * lanes, two), two), :]
                msg = message_pair(tab, idx, base + c, base + c + 1, add, lanes, top)
                acc[pl.ds(pl.multiple_of(c * lanes, two), two), :] = msg
            return carry

        lax.fori_loop(0, step // (2 * unroll), some, 0)
        agg = [acc[pl.ds(k, step, stride=lanes), :].astype(BF16) for k in range(lanes)]
        total = upd[pl.ds(base, step), :] + mm(jnp.concatenate(agg, axis=1), w_agg[...])
        if len(refs) == 3:
            refs[0][pl.ds(base, step), :] = total
            return carry
        cells_in, w_out, out = refs[:3]
        z = gate(0.5 * total).astype(BF16)
        change = lax.dot_general(w_out[...], z, (((1,), (1,)), ((), ())), preferred_element_type=F32)
        cut = pl.ds(base, step)
        out[:, cut] = (cells_in[:, cut].astype(F32) + change).astype(BF16)
        return carry

    lax.fori_loop(0, cells // step, chunk, 0)


def cells_call(idx, recv, upd, w_agg, blocks, last=(), step=1024):
    cells, width = upd.shape
    lanes = width // LANE
    shape = jax.ShapeDtypeStruct(last[0].shape, BF16) if last else jax.ShapeDtypeStruct(upd.shape, F32)
    return pl.pallas_call(
        functools.partial(cells_kernel, n_blocks=len(blocks), step=step, unroll=32),
        out_shape=shape,
        in_specs=[SM] + [VM] * (3 + len(blocks) + len(last)),
        out_specs=VM,
        scratch_shapes=[
            pltpu.VMEM((sum(b.shape[0] for b in blocks) + 4 * lanes, LANE), F32),
            pltpu.VMEM((step * lanes, LANE), F32),
        ],
        compiler_params=params(8 + len(blocks) * 2),
        cost_estimate=cost(4 * cells * width * width, 16 * cells * width, 2 * cells * width),
    )(idx, recv, upd, w_agg, *blocks, *last)


def shards(
    grid_in,
    mesh_emb,
    enc_dest,
    enc_node,
    enc_dist,
    dec_dist,
    mesh_src,
    proc_dist,
    w_grid_in,
    w_enc_src,
    w_enc_dist,
    w_mesh_self,
    w_mesh_agg,
    w_proc_send,
    w_proc_recv,
    w_proc_dist,
    w_proc_self,
    w_proc_agg,
    w_dec_send,
    w_dec_recv,
    w_dec_dist,
    w_grid_self,
    w_grid_agg,
    w_grid_out,
):
    width = w_grid_in.shape[1]
    lanes = width // LANE
    rows = mesh_emb.shape[0]
    where = (lax.axis_size("lon"), lax.axis_index("lat"), lax.axis_index("lon"))
    cells_in, dest, node = grid_in.T, enc_dest.T, enc_node.T

    enc_wd, lengths = w_enc_dist[None], enc_dist.T
    grid_h, msg1, far_key, z_own, z_pair, z_band = front_call(
        dest, node, lengths, enc_wd, w_grid_in, cells_in, w_enc_src, rows, where[0], 6
    )

    def partial(slot, messages):
        ids = slot * rows + lax.broadcasted_iota(jnp.int32, (rows, 1), 0)
        return mm((far_key == ids).astype(BF16), messages).astype(BF16)

    z_pair, z_band = across_pair(z_pair), across_band(z_band)
    z_pair, messages = with_done(z_pair, msg1)
    z_sum = (z_own.astype(F32) + z_pair.astype(F32) + z_band.astype(F32)).astype(BF16)
    p_band, p_pair = across_band(partial(5, messages)), across_pair(partial(4, messages))
    z_sum, messages, late_key = with_done(z_sum, messages, far_key)
    z_in = two_columns(z_sum, -1)
    p_own = partial(3, messages)
    p_sum = (p_own.astype(F32) + p_pair.astype(F32) + p_band.astype(F32) + z_in.astype(F32)).astype(BF16)
    o_pair, o_band = across_pair(partial(1, messages)), across_band(partial(2, messages))
    p_sum, grid_h = with_done(p_sum, grid_h)
    own = own_call(grid_h, node, lengths, w_enc_src, enc_wd, rows)
    recv0, recv1, grid_upd = cell_call(grid_h, dec_dist.T, w_dec_recv, w_grid_self, (0.5 * w_dec_dist)[None])
    source = mesh_src.T
    proc_idx = ((slot_of(source // rows, *where) * rows + source % rows) * lanes).reshape(-1)
    near_idx, far_idx = node[0] * lanes, late_key[0] * lanes - rows * lanes
    p_in, own, recv0, recv1, grid_upd, proc_idx, near_idx, far_idx = with_done(
        across_columns(p_sum), own, recv0, recv1, grid_upd, proc_idx, near_idx, far_idx
    )
    mesh_h, proc_send = mesh_call(mesh_emb, own, (o_pair, o_band, p_in), w_mesh_self, w_mesh_agg, w_proc_send)

    recv, mesh_upd = recv_call(mesh_h, proc_dist.T, w_proc_recv, w_proc_self, (0.5 * w_proc_dist)[None])
    nearby, (recv, mesh_upd) = halo(proc_send, recv, mesh_upd)
    dec_send = proc_call(proc_idx, recv, nearby, mesh_h, mesh_upd, w_proc_agg, w_dec_send)

    grid_upd = cells_call(near_idx, recv0, grid_upd, w_grid_agg, [dec_send])
    around, (grid_upd,) = halo(dec_send, grid_upd)
    pred = cells_call(far_idx, recv1, grid_upd, w_grid_agg, around[1:], (cells_in, w_grid_out.T))
    return pred.T


def solution(mesh):
    split = P(("lat", "lon"), None)
    in_specs = (split,) * 8 + (P(),) * 16
    return jax.shard_map(shards, mesh=mesh, in_specs=in_specs, out_specs=split, check_vma=False)
```

```python
import functools

import jax
import jax.numpy as jnp
from jax import lax
from jax.experimental import pallas as pl
from jax.experimental.pallas import tpu as pltpu
from jax.sharding import PartitionSpec as P

F32, BF16 = jnp.float32, jnp.bfloat16
LANE = 128
VM = pl.BlockSpec(memory_space=pltpu.VMEM)
SM = pl.BlockSpec(memory_space=pltpu.SMEM)
HB = pl.BlockSpec(memory_space=pltpu.HBM)


def mm(a, b):
    return jnp.dot(a, b, preferred_element_type=F32)


def gate(half):
    return half * jnp.tanh(half) + half


def across_pair(block):
    n = lax.axis_size("lat")
    return lax.ppermute(block, "lat", [(i, i ^ 1) for i in range(n)])


def across_band(block):
    n = lax.axis_size("lat")
    pairs = []
    for i in range(1, n - 1, 2):
        pairs += [(i, i + 1), (i + 1, i)]
    return lax.ppermute(block, "lat", pairs)


def across_columns(block):
    n = lax.axis_size("lon")
    return lax.ppermute(block, "lon", [(i, i ^ 1) for i in range(n)])


def two_columns(block, sign):
    n = lax.axis_size("lon")
    pairs = [(i, (i + (2 * sign if i % 2 == 0 else -2 * sign)) % n) for i in range(n)]
    return lax.ppermute(block, "lon", pairs)


def slot_of(patch, n_lon, my_lat, my_lon):
    row, col = patch // n_lon, patch % n_lon
    row_slot = jnp.where(row == my_lat, 0, jnp.where(row == (my_lat ^ 1), 1, 2))
    col_slot = jnp.where(col == my_lon, 0, jnp.where(col == (my_lon ^ 1), 1, 2))
    return col_slot * 3 + row_slot


def with_done(*blocks):
    return lax.optimization_barrier(blocks)


def halo(own, *work):
    *work, own_band, pair_col = with_done(*work, across_band(own), across_columns(own))
    far_col = two_columns(pair_col, 1)
    pc_band = across_band(pair_col)
    own_pair = across_pair(own)
    pc_pair = across_pair(pair_col)
    fc_band = across_band(far_col)
    fc_pair = across_pair(far_col)
    return [own, own_pair, own_band, pair_col, pc_pair, pc_band, far_col, fc_pair, fc_band], work


def params(mib):
    return pltpu.CompilerParams(vmem_limit_bytes=mib * 2**20)


def cost(flops, moved, exps=0):
    return pl.CostEstimate(flops=flops, bytes_accessed=moved, transcendentals=exps)


def grouped(full, spread, rows, lanes, every, first=0):
    for k in range(lanes):
        spread[pl.ds(first + k, rows, stride=every), :] = full[:, k * LANE : (k + 1) * LANE]


def widen(tab, base, block, step=256):
    def go(i, carry):
        r = pl.multiple_of(i * step, step)
        tab[pl.ds(base + r, step), :] = block[pl.ds(r, step), :].astype(F32)
        return carry

    lax.fori_loop(0, block.shape[0] // step, go, 0)


def around_patch(n_lon):
    row, col = lax.axis_index("lat"), lax.axis_index("lon")
    side = lax.rem(row, 2) * 2 - 1
    turn = lax.rem(col, 2) * 2 - 1
    return [
        r * n_lon + lax.rem(c + n_lon, n_lon)
        for c in (col, col - turn, col + turn)
        for r in (row, row - side, row + side)
    ]


def front_kernel(*refs, n_lon, first, step):
    ins, outs, rest = refs[:7], refs[7:13], refs[13:]
    grid_h, msg1, key, own, pair, band = rest[7:13]
    sems = rest[13]
    copies = [pltpu.make_async_copy(a, b, sems.at[n]) for n, (a, b) in enumerate(zip(ins, rest))]
    back = [pltpu.make_async_copy(a, b, sems.at[7 + n]) for n, (a, b) in enumerate(zip(rest[7:13], outs))]
    for copy in copies:
        copy.start()
    dest, node, dist, wd, w_in, cells_in, w_src = rest[:7]
    cells, width = grid_h.shape
    rows = own.shape[0]
    for copy in copies[:4]:
        copy.wait()
    slot = jnp.zeros((1, cells), jnp.int32)
    for s, patch in enumerate(around_patch(n_lon)):
        slot = jnp.where(dest[1:2, :] == patch, s, slot)
    key[...] = slot * rows + node[1:2, :]
    back[2].start()
    half_wd = 0.5 * wd[...]
    lengths = dist[...].T
    for copy in copies[4:]:
        copy.wait()
    for c in range(0, cells, step):
        cut = slice(c, c + step)
        half = 0.5 * lax.dot_general(
            cells_in[:, cut], w_in[...], (((0,), (0,)), ((), ())), preferred_element_type=F32
        )
        h = gate(half).astype(BF16)
        grid_h[cut, :] = h
        proj = 0.5 * mm(h, w_src[...])
        msg1[cut, :] = gate(proj + lengths[cut, 1:2] * half_wd).astype(BF16)
    back[0].start()
    back[1].start()
    for s, out in enumerate((own, pair, band)):
        ids = (first + s) * rows + lax.broadcasted_iota(jnp.int32, (rows, cells), 0)
        out[...] = mm((key[...] == ids).astype(BF16), msg1[...]).astype(BF16)
        back[3 + s].start()
    for copy in back:
        copy.wait()


def front_call(dest, node, dist, wd, w_in, cells_in, w_src, rows, n_lon, first, step=512):
    cells, width = cells_in.shape[1], w_in.shape[1]
    tall = jax.ShapeDtypeStruct((cells, width), BF16)
    patch = jax.ShapeDtypeStruct((rows, width), BF16)
    args = (dest, node, dist, wd, w_in, cells_in, w_src)
    shapes = (tall, tall, jax.ShapeDtypeStruct((1, cells), jnp.int32), patch, patch, patch)
    return pl.pallas_call(
        functools.partial(front_kernel, n_lon=n_lon, first=first, step=step),
        out_shape=shapes,
        in_specs=[HB] * 7,
        out_specs=(HB,) * 6,
        scratch_shapes=[pltpu.VMEM(a.shape, a.dtype) for a in args + shapes] + [pltpu.SemaphoreType.DMA((13,))],
        compiler_params=params(60),
        cost_estimate=cost(8 * rows * cells * width, 12 * cells * width, 2 * cells * width),
    )(*args)


def own_kernel(grid_h, node, dist, w_src, wd, own, msg, *, step):
    cells, width = grid_h.shape
    lengths = dist[...].T
    half_wd = 0.5 * wd[...]
    for c in range(0, cells, step):
        cut = slice(c, c + step)
        proj = 0.5 * mm(grid_h[cut, :], w_src[...])
        msg[cut, :] = gate(proj + lengths[cut, 0:1] * half_wd).astype(BF16)
    ids = lax.broadcasted_iota(jnp.int32, (own.shape[0], cells), 0)
    own[...] = mm((node[0:1, :] == ids).astype(BF16), msg[...])


def own_call(grid_h, node, dist, w_src, wd, rows, step=256):
    cells, width = grid_h.shape
    return pl.pallas_call(
        functools.partial(own_kernel, step=step),
        out_shape=jax.ShapeDtypeStruct((rows, width), F32),
        in_specs=[VM] * 5,
        out_specs=VM,
        scratch_shapes=[pltpu.VMEM((cells, width), BF16)],
        compiler_params=params(12),
        cost_estimate=cost(4 * rows * cells * width, 6 * cells * width, cells * width),
    )(grid_h, node, dist, w_src, wd)


def mesh_kernel(emb, own, s0, s1, s2, w_self, w_agg, w_send, mesh_h, send, spread):
    rows, width = emb.shape
    agg = own[...]
    for part in (s0, s1, s2):
        agg += part[...].astype(F32)
    agg = agg.astype(BF16)
    upd = mm(emb[...], w_self[...]) + mm(agg, w_agg[...])
    h = (emb[...].astype(F32) + gate(0.5 * upd)).astype(BF16)
    mesh_h[...] = h
    grouped(0.5 * mm(h, w_send[...]), spread, rows, width // LANE, width // LANE)
    send[...] = spread[...].astype(BF16)


def mesh_call(emb, own, sums, w_self, w_agg, w_send):
    rows, width = emb.shape
    flat = (rows * width // LANE, LANE)
    return pl.pallas_call(
        mesh_kernel,
        out_shape=(jax.ShapeDtypeStruct((rows, width), BF16), jax.ShapeDtypeStruct(flat, BF16)),
        in_specs=[VM] * 8,
        out_specs=(VM, VM),
        scratch_shapes=[pltpu.VMEM(flat, F32)],
        compiler_params=params(8),
        cost_estimate=cost(6 * rows * width * width, 16 * rows * width, rows * width),
    )(emb, own, *sums, w_self, w_agg, w_send)


def recv_kernel(mesh_h, dist, w_recv, w_self, wd, recv, upd):
    rows, width = mesh_h.shape
    lanes = width // LANE
    degree = dist.shape[0]
    half = 0.5 * mm(mesh_h[...], w_recv[...])
    lengths = dist[...].T
    for j in range(degree):
        grouped(half + lengths[:, j : j + 1] * wd[...], recv, rows, lanes, degree * lanes, j * lanes)
    upd[...] = mm(mesh_h[...], w_self[...])


def recv_call(mesh_h, dist, w_recv, w_self, wd):
    rows, width = mesh_h.shape
    degree = dist.shape[0]
    return pl.pallas_call(
        recv_kernel,
        out_shape=(
            jax.ShapeDtypeStruct((rows * degree * width // LANE, LANE), F32),
            jax.ShapeDtypeStruct((rows, width), F32),
        ),
        in_specs=[VM] * 5,
        out_specs=(VM, VM),
        compiler_params=params(8),
        cost_estimate=cost(4 * rows * width * width, 40 * rows * width),
    )(mesh_h, dist, w_recv, w_self, wd)


def message_pair(tab, idx, a, b, recv, lanes, top):
    first = tab[pl.ds(idx[a] + 2 * lanes, 2 * lanes), :]
    second = tab[pl.ds(idx[b] + lanes, 2 * lanes), :]
    return gate(jnp.where(top, first, second) + recv)


def proc_kernel(idx, recv, *refs, unroll):
    blocks, (mesh_h, upd, w_agg, w_send, out, tab, acc) = refs[:9], refs[9:]
    rows, width = mesh_h.shape
    lanes = width // LANE
    two = 2 * lanes
    degree = idx.shape[0] // rows
    for s, b in enumerate(blocks):
        widen(tab, lanes * (2 + s * rows), b)
    top = lax.broadcasted_iota(jnp.int32, (two, LANE), 0) < lanes

    def node(n):
        total = None
        for j in range(0, degree, 2):
            add = recv[pl.ds(pl.multiple_of((n * degree + j) * lanes, two), two), :]
            msg = message_pair(tab, idx, j * rows + n, (j + 1) * rows + n, add, lanes, top)
            total = msg if total is None else total + msg
        acc[pl.ds(pl.multiple_of(n * two, two), two), :] = total

    def some(i, carry):
        for u in range(unroll):
            node(i * unroll + u)
        return carry

    lax.fori_loop(0, rows // unroll, some, 0)
    agg = [
        (acc[pl.ds(k, rows, stride=two), :] + acc[pl.ds(k + lanes, rows, stride=two), :]).astype(BF16)
        for k in range(lanes)
    ]
    total = upd[...] + mm(jnp.concatenate(agg, axis=1), w_agg[...])
    mesh_out = (mesh_h[...].astype(F32) + gate(0.5 * total)).astype(BF16)
    spread = acc.at[pl.ds(0, rows * lanes), :]
    grouped(0.5 * mm(mesh_out, w_send[...]), spread, rows, lanes, lanes)
    out[...] = spread[...].astype(BF16)


def proc_call(idx, recv, blocks, mesh_h, upd, w_agg, w_send):
    rows, width = mesh_h.shape
    lanes = width // LANE
    return pl.pallas_call(
        functools.partial(proc_kernel, unroll=16),
        out_shape=jax.ShapeDtypeStruct((rows * lanes, LANE), BF16),
        in_specs=[SM] + [VM] * 14,
        out_specs=VM,
        scratch_shapes=[
            pltpu.VMEM((lanes * (9 * rows + 4), LANE), F32),
            pltpu.VMEM((rows * 2 * lanes, LANE), F32),
        ],
        compiler_params=params(16),
        cost_estimate=cost(4 * rows * width * width, 32 * rows * width, idx.size * width),
    )(idx, recv, *blocks, mesh_h, upd, w_agg, w_send)


def cell_kernel(grid_h, dist, w_recv, w_self, wd, recv0, recv1, upd, *, step):
    cells, width = grid_h.shape
    lanes = width // LANE
    lengths = dist[...].T
    for c in range(0, cells, step):
        cut = slice(c, c + step)
        half = 0.5 * mm(grid_h[cut, :], w_recv[...])
        for k, recv in enumerate((recv0, recv1)):
            grouped(half + lengths[cut, k : k + 1] * wd[...], recv, step, lanes, lanes, c * lanes)
        upd[cut, :] = mm(grid_h[cut, :], w_self[...])


def cell_call(grid_h, dist, w_recv, w_self, wd, step=256):
    cells, width = grid_h.shape
    lanes = width // LANE
    flat = jax.ShapeDtypeStruct((cells * lanes, LANE), F32)
    return pl.pallas_call(
        functools.partial(cell_kernel, step=step),
        out_shape=(flat, flat, jax.ShapeDtypeStruct((cells, width), F32)),
        in_specs=[VM] * 5,
        out_specs=(VM,) * 3,
        compiler_params=params(8),
        cost_estimate=cost(4 * cells * width * width, 14 * cells * width),
    )(grid_h, dist, w_recv, w_self, wd)


def cells_kernel(idx, recv, upd, w_agg, *refs, n_blocks, step, unroll):
    blocks, refs = refs[:n_blocks], refs[n_blocks:]
    tab, acc = refs[-2:]
    cells, width = upd.shape
    lanes = width // LANE
    two = 2 * lanes
    size = blocks[0].shape[0]
    for s, b in enumerate(blocks):
        widen(tab, two + s * size, b)
    top = lax.broadcasted_iota(jnp.int32, (two, LANE), 0) < lanes

    def chunk(i, carry):
        base = pl.multiple_of(i * step, step)

        def some(q, carry):
            for u in range(unroll):
                c = (q * unroll + u) * 2
                add = recv[pl.ds(pl.multiple_of((base + c) * lanes, two), two), :]
                msg = message_pair(tab, idx, base + c, base + c + 1, add, lanes, top)
                acc[pl.ds(pl.multiple_of(c * lanes, two), two), :] = msg
            return carry

        lax.fori_loop(0, step // (2 * unroll), some, 0)
        agg = [acc[pl.ds(k, step, stride=lanes), :].astype(BF16) for k in range(lanes)]
        total = upd[pl.ds(base, step), :] + mm(jnp.concatenate(agg, axis=1), w_agg[...])
        if len(refs) == 3:
            refs[0][pl.ds(base, step), :] = total
            return carry
        cells_in, w_out, out = refs[:3]
        z = gate(0.5 * total).astype(BF16)
        change = lax.dot_general(w_out[...], z, (((1,), (1,)), ((), ())), preferred_element_type=F32)
        cut = pl.ds(base, step)
        out[:, cut] = (cells_in[:, cut].astype(F32) + change).astype(BF16)
        return carry

    lax.fori_loop(0, cells // step, chunk, 0)


def cells_call(idx, recv, upd, w_agg, blocks, last=(), step=1024):
    cells, width = upd.shape
    lanes = width // LANE
    shape = jax.ShapeDtypeStruct(last[0].shape, BF16) if last else jax.ShapeDtypeStruct(upd.shape, F32)
    return pl.pallas_call(
        functools.partial(cells_kernel, n_blocks=len(blocks), step=step, unroll=32),
        out_shape=shape,
        in_specs=[SM] + [VM] * (3 + len(blocks) + len(last)),
        out_specs=VM,
        scratch_shapes=[
            pltpu.VMEM((sum(b.shape[0] for b in blocks) + 4 * lanes, LANE), F32),
            pltpu.VMEM((step * lanes, LANE), F32),
        ],
        compiler_params=params(8 + len(blocks) * 2),
        cost_estimate=cost(4 * cells * width * width, 16 * cells * width, 2 * cells * width),
    )(idx, recv, upd, w_agg, *blocks, *last)


def shards(
    grid_in,
    mesh_emb,
    enc_dest,
    enc_node,
    enc_dist,
    dec_dist,
    mesh_src,
    proc_dist,
    w_grid_in,
    w_enc_src,
    w_enc_dist,
    w_mesh_self,
    w_mesh_agg,
    w_proc_send,
    w_proc_recv,
    w_proc_dist,
    w_proc_self,
    w_proc_agg,
    w_dec_send,
    w_dec_recv,
    w_dec_dist,
    w_grid_self,
    w_grid_agg,
    w_grid_out,
):
    width = w_grid_in.shape[1]
    lanes = width // LANE
    rows = mesh_emb.shape[0]
    where = (lax.axis_size("lon"), lax.axis_index("lat"), lax.axis_index("lon"))
    cells_in, dest, node = grid_in.T, enc_dest.T, enc_node.T

    enc_wd, lengths = w_enc_dist[None], enc_dist.T
    grid_h, msg1, far_key, z_own, z_pair, z_band = front_call(
        dest, node, lengths, enc_wd, w_grid_in, cells_in, w_enc_src, rows, where[0], 6
    )

    def partial(slot, messages):
        ids = slot * rows + lax.broadcasted_iota(jnp.int32, (rows, 1), 0)
        return mm((far_key == ids).astype(BF16), messages).astype(BF16)

    z_pair, z_band = across_pair(z_pair), across_band(z_band)
    z_pair, messages = with_done(z_pair, msg1)
    z_sum = (z_own.astype(F32) + z_pair.astype(F32) + z_band.astype(F32)).astype(BF16)
    p_band, p_pair = across_band(partial(5, messages)), across_pair(partial(4, messages))
    z_sum, messages, late_key = with_done(z_sum, messages, far_key)
    z_in = two_columns(z_sum, -1)
    p_own = partial(3, messages)
    p_sum = (p_own.astype(F32) + p_pair.astype(F32) + p_band.astype(F32) + z_in.astype(F32)).astype(BF16)
    o_pair, o_band = across_pair(partial(1, messages)), across_band(partial(2, messages))
    p_sum, grid_h = with_done(p_sum, grid_h)
    own = own_call(grid_h, node, lengths, w_enc_src, enc_wd, rows)
    recv0, recv1, grid_upd = cell_call(grid_h, dec_dist.T, w_dec_recv, w_grid_self, (0.5 * w_dec_dist)[None])
    source = mesh_src.T
    proc_idx = ((slot_of(source // rows, *where) * rows + source % rows) * lanes).reshape(-1)
    near_idx, far_idx = node[0] * lanes, late_key[0] * lanes - rows * lanes
    p_in, own, recv0, recv1, grid_upd, proc_idx, near_idx, far_idx = with_done(
        across_columns(p_sum), own, recv0, recv1, grid_upd, proc_idx, near_idx, far_idx
    )
    mesh_h, proc_send = mesh_call(mesh_emb, own, (o_pair, o_band, p_in), w_mesh_self, w_mesh_agg, w_proc_send)

    recv, mesh_upd = recv_call(mesh_h, proc_dist.T, w_proc_recv, w_proc_self, (0.5 * w_proc_dist)[None])
    nearby, (recv, mesh_upd) = halo(proc_send, recv, mesh_upd)
    dec_send = proc_call(proc_idx, recv, nearby, mesh_h, mesh_upd, w_proc_agg, w_dec_send)

    grid_upd = cells_call(near_idx, recv0, grid_upd, w_grid_agg, [dec_send])
    around, (grid_upd,) = halo(dec_send, grid_upd)
    pred = cells_call(far_idx, recv1, grid_upd, w_grid_agg, around[1:], (cells_in, w_grid_out.T))
    return pred.T


def solution(mesh):
    split = P(("lat", "lon"), None)
    in_specs = (split,) * 8 + (P(),) * 16
    return jax.shard_map(shards, mesh=mesh, in_specs=in_specs, out_specs=split, check_vma=False)
```
